512 devices in a mesh: pair: 2 (over core), latent: 32 (over x, z_lo), tok: 8 (over y, z_hi).
Axes of the slice: x: 4, y: 4, z: 16 (z_hi: 2, z_lo: 8; z = z_hi * 8 + z_lo), core: 2. Of those that a mesh axis runs over, the one named last changes fastest.
Arguments:
- activations: bfloat16 [2, 512, 3584], P('pair', 'tok'), may hold values from -6 to 6
- enc_weight: bfloat16 [2, 3584, 65536], P('pair', None, ('latent', 'tok')), may hold values from -0.0625 to 0.0625
- enc_bias: float32 [65536], P(('latent', 'tok')), may hold values from -3 to 3
- thresholds: int32 [65536], P(('latent', 'tok')), may hold values from 1 to 4
- dec_weight: bfloat16 [2, 65536, 3584], P('pair', 'latent', 'tok'), may hold values from -0.0234375 to 0.0234375
- dec_bias: float32 [2, 3584], P('pair', 'tok'), may hold values from -3 to 3
Outputs:
- recon: bfloat16 [2, 512, 3584], P('pair', 'latent', 'tok')
- token_loss: float32 [512], P('latent')
- scaling: float32 [2, 65536], P('pair', ('latent', 'tok'))
The draws below stay inside these ranges and needn't reach their ends.
All inputs are finite; a program needn't handle non-finite values.
Results may differ from the reference program's by a relative error of at most 0.017.
Values may be sent and summed in bfloat16 or wider, within the bound.
No kernel may reach another device: no remote copies, remote signals or barrier semaphores. Data moves between devices by JAX's collectives and lax.ppermute only.
A program may use at most 64 MiB of HBM per device.

```python
import jax
import jax.numpy as jnp
from jax import lax

D = 3584
L = 65536
TOKENS = 512


def place_ends(array, key, smallest, top_value):
    shape = array.shape
    index_at = [jax.random.randint(jax.random.fold_in(key, axis), (), 0, shape[axis]) for axis in range(len(shape))]
    array = array.at[tuple(index_at)].set(smallest)
    longest = shape.index(max(shape))
    index_at[longest] = (index_at[longest] + 1) % shape[longest]
    return array.at[tuple(index_at)].set(top_value)


def steps_of(stream_key, extent, cuts, least, largest):
    loudness, own = 1.0, jax.random.fold_in(stream_key, 6)
    for axis_at, shards_of in cuts:
        steps = jnp.exp(jax.random.uniform(jax.random.fold_in(own, axis_at), (shards_of,), jnp.float32, least / len(cuts), largest / len(cuts)))
        loudness = loudness * jnp.repeat(steps, extent[axis_at] // shards_of).reshape([-1 if axis == axis_at else 1 for axis in range(len(extent))])
    return loudness


def centred(stream_key, shape, width, limit, shards=(), kind=jnp.bfloat16):
    factor_of = steps_of(stream_key, shape, shards, -0.22, 0.18) if shards else 1.0
    drawn = jax.random.normal(stream_key, shape, jnp.float32) * width * factor_of
    return jnp.minimum(jnp.maximum(drawn, -limit), limit).astype(kind)


def setup_inputs(seed: int = 0) -> dict:
    arg_keys = jax.random.split(jax.random.key(seed), 7)
    return {
        "activations": centred(arg_keys[0], (2, TOKENS, D), 1.0, 6.0, ((0, 2), (1, 8))),
        "enc_weight": centred(arg_keys[1], (2, D, L), (2 * D) ** -0.5, 0.0625, ((0, 2), (2, 256))),
        "enc_bias": centred(arg_keys[2], (L,), 0.5, 3.0, ((0, 256),), jnp.float32),
        "thresholds": place_ends(jax.random.randint(arg_keys[3], (L,), 1, 5), jax.random.fold_in(arg_keys[3], 1), 1, 4).astype(jnp.int32),
        "dec_weight": centred(arg_keys[4], (2, L, D), L ** -0.5, 0.0234375, ((0, 2), (1, 32), (2, 8))),
        "dec_bias": centred(arg_keys[5], (2, D), 0.5, 3.0, ((0, 2), (1, 8)), jnp.float32),
    }


smooth_width = 0.1
penalty = 0.0001
tiny_term = 1e-06

def reference(activations, enc_weight, enc_bias, thresholds, dec_weight, dec_bias):
    pre = jnp.dot(activations[0], enc_weight[0], preferred_element_type=jnp.float32)
    pre = pre + jnp.dot(activations[1], enc_weight[1], preferred_element_type=jnp.float32)
    pre = pre + enc_bias
    thresh_level = thresholds.astype(jnp.float32) * 0.25
    features = (pre * jax.nn.sigmoid((pre - thresh_level) / smooth_width)).astype(jnp.bfloat16)
    feat_wide = features.astype(jnp.float32)
    mean_sq = lax.optimization_barrier(jnp.mean(feat_wide * feat_wide, axis=0))
    recon_list = []
    scale_list = []
    sq_error = jnp.zeros((features.shape[0],), jnp.float32)
    sparse = jnp.zeros((features.shape[0],), jnp.float32)
    for model in range(2):
        recon_vals = jnp.dot(features, dec_weight[model], preferred_element_type=jnp.float32) + dec_bias[model]
        residue = activations[model].astype(jnp.float32) - recon_vals
        sq_error = sq_error + lax.optimization_barrier(jnp.sum(residue * residue, axis=1))
        recon_list.append(recon_vals.astype(jnp.bfloat16))
        dec_wide = dec_weight[model].astype(jnp.float32)
        norm_sq = lax.optimization_barrier(jnp.sum(dec_wide * dec_wide, axis=1))
        sparse = sparse + lax.optimization_barrier(jnp.sum(feat_wide * jnp.sqrt(norm_sq), axis=1))
        inner_prod = lax.dot_general(activations[model], dec_weight[model], (((1,), (1,)), ((), ())), preferred_element_type=jnp.float32)
        numer = lax.optimization_barrier(jnp.sum(feat_wide * inner_prod, axis=0)) / features.shape[0]
        scale_list.append(numer / (norm_sq * mean_sq + tiny_term))
    token_loss = sq_error / (2.0 * D) + penalty * sparse
    return (jnp.stack(recon_list), token_loss, jnp.stack(scale_list))
```

```python
import jax
import jax.numpy as jnp
from jax import lax
from jax.sharding import Mesh, PartitionSpec as P

D = 3584
smooth_width = 0.1
penalty = 0.0001
tiny_term = 1e-06
LAT = ("x", "zl")
TOK = ("y", "zh")
BF = jnp.bfloat16
F32 = jnp.float32


def shift(value, axis, step):
    size = lax.axis_size(axis)
    return lax.ppermute(value, axis, [(i, (i + step) % size) for i in range(size)])


def ring_blocks(block):
    half = block.shape[0] // 2
    prev = shift(block, "y", 1)
    succ = shift(block, "y", -1)
    far_top = shift(prev[:half], "y", 1)
    far_low = shift(succ[half:], "y", -1)
    return [block, prev, succ, jnp.concatenate([far_top, far_low], axis=0)]


def body(activations, enc_weight, enc_bias, thresholds, dec_weight, dec_bias):
    y_at = lax.axis_index("y")
    zh_at = lax.axis_index("zh")
    tok_at = y_at * 2 + zh_at
    lat_at = lax.axis_index(LAT)
    act = activations[0]
    enc = enc_weight[0]
    dec = dec_weight[0]
    count = act.shape[0]
    own = enc.shape[1]
    width = dec.shape[1]
    places = [y_at, (y_at + 3) % 4, (y_at + 1) % 4, (y_at + 2) % 4]

    other_act = shift(act, "zh", 1)
    near = jnp.concatenate(ring_blocks(act), axis=0)
    far = jnp.concatenate(ring_blocks(other_act), axis=0)

    dec_wide = dec.astype(F32)
    nsq_part = jnp.sum(dec_wide * dec_wide, axis=1)
    nsq_own = jnp.sum(
        lax.all_to_all(nsq_part.reshape(8, own), TOK, 0, 0, tiled=True), axis=0
    )
    norm_own = jnp.sqrt(nsq_own)

    pre_near = jnp.dot(near, enc, preferred_element_type=F32)
    pre_far = jnp.dot(far, enc, preferred_element_type=F32)

    def in_order(from_near, from_far):
        cols = from_near.shape[1]
        out = jnp.zeros((8 * count, cols), from_near.dtype)
        for part, half_at in ((from_near, zh_at), (from_far, 1 - zh_at)):
            for k, place in enumerate(places):
                out = lax.dynamic_update_slice(
                    out, part[k * count : (k + 1) * count], ((place * 2 + half_at) * count, 0)
                )
        return out

    partial_value = in_order(pre_near, pre_far)
    thresh_level = thresholds.astype(F32) * 0.25
    pre = partial_value + shift(partial_value, "pair", 1) + enc_bias
    feats = (pre * jax.nn.sigmoid((pre - thresh_level) / smooth_width)).astype(BF)
    feats_wide = feats.astype(F32)
    mean_sq = jnp.mean(feats_wide * feats_wide, axis=0)
    sparse_part = jnp.sum(feats_wide * norm_own, axis=1)

    act_slice = in_order(
        lax.dynamic_slice_in_dim(near, tok_at * width, width, 1),
        lax.dynamic_slice_in_dim(far, tok_at * width, width, 1),
    )

    other_feats = shift(feats, "zh", 1)
    blocks_near = ring_blocks(feats)
    blocks_far = ring_blocks(other_feats)
    block_feats = jnp.zeros((8 * count, 8 * own), BF)
    for blocks, half_at in ((blocks_near, zh_at), (blocks_far, 1 - zh_at)):
        for place, blk in zip(places, blocks):
            block_feats = lax.dynamic_update_slice(
                block_feats, blk, (0, (place * 2 + half_at) * own)
            )

    recon_part = jnp.dot(block_feats, dec, preferred_element_type=F32).astype(BF)
    sparse_hi = sparse_part.astype(BF)
    sparse_lo = (sparse_part - sparse_hi.astype(F32)).astype(BF)
    payload = jnp.concatenate(
        [
            recon_part,
            sparse_hi[:, None],
            sparse_lo[:, None],
            jnp.zeros((8 * count, 62), BF),
        ],
        axis=1,
    )
    arrived = lax.all_to_all(payload, LAT, 0, 0, tiled=True)

    inner_prod = lax.dot_general(
        act_slice, dec, (((1,), (1,)), ((), ())), preferred_element_type=F32
    )
    num_part = jnp.sum(inner_prod * block_feats.astype(F32), axis=0)

    row_count = 8 * count // lax.axis_size(LAT)
    total = jnp.sum(arrived.reshape(32, row_count, 512).astype(F32), axis=0)
    recon_vals = total[:, :width] + dec_bias[0]
    sparse = total[:, width] + total[:, width + 1]
    act_own = lax.dynamic_slice_in_dim(act_slice, lat_at * row_count, row_count, 0)
    residue = act_own.astype(F32) - recon_vals
    own_terms = jnp.sum(residue * residue, axis=1) / (2.0 * D) + penalty * sparse

    last = jnp.concatenate(
        [
            jnp.broadcast_to(num_part.reshape(1, 8, own), (2, 8, own)),
            jnp.broadcast_to(own_terms, (2, 8, row_count)),
        ],
        axis=2,
    ).reshape(16, own + row_count)
    got = lax.all_to_all(last, ("pair",) + TOK, 0, 0, tiled=True)
    token_loss = jnp.sum(got[:, own:], axis=0)
    mine = lax.dynamic_slice_in_dim(got, lax.axis_index("pair") * 8, 8, 0)[:, :own]
    num_own = jnp.sum(mine, axis=0) / (8 * count)
    scaling = num_own / (nsq_own * mean_sq + tiny_term)
    return (recon_vals.astype(BF)[None], token_loss, scaling[None])


def solution(mesh):
    fine = Mesh(mesh.devices.reshape(2, 4, 8, 4, 2), ("pair", "x", "zl", "y", "zh"))
    return jax.shard_map(
        body,
        mesh=fine,
        in_specs=(
            P("pair", TOK, None),
            P("pair", None, LAT + TOK),
            P(LAT + TOK),
            P(LAT + TOK),
            P("pair", LAT, TOK),
            P("pair", TOK),
        ),
        out_specs=(P("pair", LAT, TOK), P(LAT), P("pair", LAT + TOK)),
        check_vma=False,
    )
```

```python
import jax
import jax.numpy as jnp
from jax import lax
from jax.experimental import pallas as pl
from jax.experimental.pallas import tpu as pltpu
from jax.sharding import Mesh, PartitionSpec as P

D = 3584
smooth_width = 0.1
penalty = 0.0001
tiny_term = 1e-06
LAT = ("x", "zl")
TOK = ("y", "zh")
BF = jnp.bfloat16
F32 = jnp.float32
VMEM = pl.BlockSpec(memory_space=pltpu.VMEM)
SMEM = pl.BlockSpec(memory_space=pltpu.SMEM)
NT = (((1,), (1,)), ((), ()))


def swap(value, axis):
    return lax.ppermute(value, axis, [(0, 1), (1, 0)])


def gather(value, axes):
    size = lax.axis_size(axes)
    copies = jnp.broadcast_to(value[None], (size,) + value.shape)
    return lax.all_to_all(copies, axes, 0, 0, tiled=False)


def encode(at_ref, a_ref, enc_ref, keep_ref, send_ref, cols_ref, v_ref):
    pair_at, tok_at = at_ref[0], at_ref[2]
    v_ref[...] = jnp.dot(a_ref[...], enc_ref[...], preferred_element_type=F32)
    keep_ref[...] = v_ref[pl.ds(pl.multiple_of(pair_at * 128, 128), 128), :]
    send_ref[...] = v_ref[pl.ds(pl.multiple_of((1 - pair_at) * 128, 128), 128), :]
    base = (tok_at // 2) * 896 + (tok_at % 2) * 384
    window = a_ref[:, pl.ds(pl.multiple_of(base, 128), 512)]
    cols_ref[...] = jnp.where(tok_at % 2 == 1, window[:, 64:512], window[:, 0:448])


def near_kernel(at_ref, b0, b1, b2, b3, enc_ref, keep_ref, send_ref, cols_ref, a_ref, v_ref):
    y_at = at_ref[3]
    for ref, step in ((b0, 0), (b1, 3), (b2, 1), (b3, 2)):
        row = pl.multiple_of(((y_at + step) % 4) * 64, 64)
        a_ref[pl.ds(row, 64), :] = ref[...]
    encode(at_ref, a_ref, enc_ref, keep_ref, send_ref, cols_ref, v_ref)


def far_kernel(at_ref, a_ref, enc_ref, keep_ref, send_ref, cols_ref, v_ref):
    encode(at_ref, a_ref, enc_ref, keep_ref, send_ref, cols_ref, v_ref)


def decode_kernel(
    at_ref, g1, g2, p1, p2, dec_ref, out_ref, f_ref, nsq_ref, wide_ref, norm_ref
):
    pair_at, zh_at = at_ref[0], at_ref[1]

    nsq = jnp.zeros((8, 256), F32)
    for y in range(4):
        rows = g1[y, 384:400, :].astype(F32)
        nsq = nsq + (rows[0:8] + rows[8:16])
    nsq_ref[...] = nsq
    norm = jnp.sqrt(nsq) * 0.125
    high = norm.astype(BF).astype(F32)
    wide_ref[...] = jnp.zeros_like(wide_ref)
    for k in range(8):
        wide_ref[0:1, k * 256 : (k + 1) * 256] = high[k : k + 1]
        wide_ref[1:2, k * 256 : (k + 1) * 256] = (norm - high)[k : k + 1]
    norm_ref[...] = wide_ref[...].astype(BF)

    def place(half, own, oth):
        near = pl.multiple_of(half * 256 + zh_at * 128, 128)
        far = pl.multiple_of(half * 256 + (1 - zh_at) * 128, 128)
        for y in range(4):
            mine = pl.multiple_of((2 * y + zh_at) * 256, 256)
            theirs = pl.multiple_of((2 * y + 1 - zh_at) * 256, 256)
            f_ref[pl.ds(near, 128), pl.ds(mine, 256)] = own[y, 0:128, :]
            f_ref[pl.ds(far, 128), pl.ds(theirs, 256)] = own[y, 128:256, :]
            f_ref[pl.ds(far, 128), pl.ds(mine, 256)] = own[y, 256:384, :]
            f_ref[pl.ds(near, 128), pl.ds(theirs, 256)] = oth[y]

    place(pair_at, g1, g2)
    place(1 - pair_at, p1, p2)
    for half in range(2):
        feats = f_ref[half * 256 : (half + 1) * 256, :]
        value = lax.dot_general(feats, dec_ref[...], NT, preferred_element_type=F32)
        sparse = lax.dot_general(feats, norm_ref[...], NT, preferred_element_type=F32)
        value, sparse = value.astype(BF), sparse.astype(BF)
        for zh in range(2):
            for yy in range(2):
                src = (zh * 2 + yy) * 64
                dst = ((half * 2 + yy) * 2 + zh) * 64
                out_ref[dst : dst + 64, 0:448] = value[src : src + 64, :]
                out_ref[dst : dst + 64, 448:512] = sparse[src : src + 64, :]


def numer_kernel(at_ref, f_ref, near_ref, far_ref, dec_ref, num_ref, msq_ref, a_ref):
    zh_at, tok_at = at_ref[1], at_ref[2]
    for half in range(2):
        near = pl.multiple_of(half * 256 + zh_at * 128, 128)
        far = pl.multiple_of(half * 256 + (1 - zh_at) * 128, 128)
        a_ref[pl.ds(near, 128), :] = near_ref[half * 128 : (half + 1) * 128, :]
        a_ref[pl.ds(far, 128), :] = far_ref[half * 128 : (half + 1) * 128, :]
    for k in range(8):
        cols = slice(k * 256, (k + 1) * 256)
        inner = jnp.dot(a_ref[...], dec_ref[:, cols], preferred_element_type=F32)
        num_ref[k : k + 1, :] = jnp.sum(
            inner * f_ref[:, cols].astype(F32), axis=0, keepdims=True
        )
    own = f_ref[:, pl.ds(pl.multiple_of(tok_at * 256, 256), 256)].astype(F32)
    msq_ref[...] = jnp.sum(own * own, axis=0, keepdims=True)


def call(kernel, name, flops, outs, count, scratch):
    return pl.pallas_call(
        kernel,
        out_shape=tuple(jax.ShapeDtypeStruct(shape, kind) for shape, kind in outs),
        in_specs=[SMEM] + [VMEM] * count,
        out_specs=(VMEM,) * len(outs),
        scratch_shapes=[pltpu.VMEM(shape, kind) for shape, kind in scratch],
        compiler_params=pltpu.CompilerParams(vmem_limit_bytes=40 << 20),
        cost_estimate=pl.CostEstimate(
            flops=flops, bytes_accessed=6 << 20, transcendentals=0
        ),
        name=name,
    )


def body(activations, enc_weight, enc_bias, thresholds, dec_weight, dec_bias):
    pair_at = lax.axis_index("pair")
    x_at = lax.axis_index("x")
    zh_at = lax.axis_index("zh")
    tok_at = lax.axis_index(TOK)
    lat_at = lax.axis_index(LAT)
    act = activations[0]
    enc = enc_weight[0]
    dec = dec_weight[0]
    dec_t = dec.T
    own, width = enc.shape[1], dec.shape[1]
    tokens = 8 * act.shape[0]
    rows = tokens // lax.axis_size(LAT)
    at = jnp.stack([pair_at, zh_at, tok_at, lax.axis_index("y")]).astype(jnp.int32)

    quarter = swap(lax.dynamic_slice_in_dim(act, x_at * 16, 16, 0), "zh")
    blocks = [act] + [
        lax.ppermute(act, "y", [(i, (i + k) % 4) for i in range(4)]) for k in (1, 3, 2)
    ]
    quarter, blocks[1], blocks[2] = lax.optimization_barrier((quarter, blocks[1], blocks[2]))
    far = gather(quarter, ("y", "x")).reshape(256, D)

    dec_wide = dec.astype(F32)
    nsq_part = jnp.sum(dec_wide * dec_wide, axis=1).reshape(8, own)

    def split(value):
        high = value.astype(BF)
        return [high, (value - high.astype(F32)).astype(BF)]

    thresh_level = thresholds.astype(F32) * 0.25

    def features(keep, send):
        pre = keep + swap(send, "pair") + enc_bias
        return (pre * jax.nn.sigmoid((pre - thresh_level) / smooth_width)).astype(BF)

    enc_outs = [((128, own), F32), ((128, own), F32), ((256, width), BF)]
    enc_flops = 2 * 256 * D * own
    half_value = ((256, own), F32)
    keep, send, near_cols = call(
        near_kernel, "near", enc_flops, enc_outs, 5, [((256, D), BF), half_value]
    )(at, *blocks, enc)
    feats_near = features(keep, send)
    over = swap(jnp.concatenate([feats_near] + split(nsq_part), axis=0), "zh")
    over_near = over[:128]
    nsq_both = nsq_part + over[128:136].astype(F32) + over[136:144].astype(F32)

    keep, send, far_cols = call(far_kernel, "far", enc_flops, enc_outs, 2, [half_value])(
        at, far, enc
    )
    feats_far = features(keep, send)
    over_far = swap(feats_far, "zh")
    g1 = gather(
        jnp.concatenate([feats_near, over_near, feats_far] + split(nsq_both), axis=0), "y"
    )
    g2 = gather(over_far, "y")
    p1 = swap(g1, "pair")
    p2 = swap(g2, "pair")

    payload, block_feats, nsq_all = call(
        decode_kernel,
        "decode",
        2 * tokens * 8 * own * 512,
        [((tokens, 512), BF), ((tokens, 8 * own), BF), ((8, own), F32)],
        5,
        [((64, 8 * own), F32), ((64, 8 * own), BF)],
    )(at, g1, g2, p1, p2, dec_t)
    nsq_own = lax.dynamic_index_in_dim(nsq_all, tok_at, 0, keepdims=False)
    arrived = lax.all_to_all(payload, LAT, 0, 0, tiled=True)

    num_part, sum_sq = call(
        numer_kernel,
        "numer",
        2 * tokens * 8 * own * width,
        [((8, own), F32), ((1, own), F32)],
        4,
        [((tokens, width), BF)],
    )(at, block_feats, near_cols, far_cols, dec_t)
    mean_sq = sum_sq[0] / tokens

    total = jnp.sum(arrived.reshape(32, rows, 512).astype(F32), axis=0)
    recon_vals = total[:, :width] + dec_bias[0]
    sparse = total[:, width] + total[:, width + 1]
    own_row = (lat_at // 8) * 64 + (lat_at % 4) * rows
    act_own = jnp.where(
        (lat_at // 4) % 2 == zh_at,
        lax.dynamic_slice_in_dim(near_cols, own_row, rows, 0),
        lax.dynamic_slice_in_dim(far_cols, own_row, rows, 0),
    )
    residue = act_own.astype(F32) - recon_vals
    own_terms = jnp.sum(residue * residue, axis=1) / (2.0 * D) + penalty * sparse

    last = jnp.concatenate(
        [
            jnp.broadcast_to(num_part.reshape(1, 8, own), (2, 8, own)),
            jnp.broadcast_to(own_terms, (2, 8, rows)),
        ],
        axis=2,
    ).reshape(16, own + rows)
    got = lax.all_to_all(last, ("pair",) + TOK, 0, 0, tiled=True)
    token_loss = jnp.sum(got[:, own:], axis=0)
    mine = lax.dynamic_slice_in_dim(got, pair_at * 8, 8, 0)[:, :own]
    num_own = jnp.sum(mine, axis=0) / tokens
    scaling = num_own / (nsq_own * mean_sq + tiny_term)
    return (recon_vals.astype(BF)[None], token_loss, scaling[None])


def solution(mesh):
    fine = Mesh(mesh.devices.reshape(2, 4, 8, 4, 2), ("pair", "x", "zl", "y", "zh"))
    return jax.shard_map(
        body,
        mesh=fine,
        in_specs=(
            P("pair", TOK, None),
            P("pair", None, LAT + TOK),
            P(LAT + TOK),
            P(LAT + TOK),
            P("pair", LAT, TOK),
            P("pair", TOK),
        ),
        out_specs=(P("pair", LAT, TOK), P(LAT), P("pair", LAT + TOK)),
        check_vma=False,
    )
```

```python
import jax
import jax.numpy as jnp
from jax import lax
from jax.experimental import pallas as pl
from jax.experimental.pallas import tpu as pltpu
from jax.sharding import Mesh, PartitionSpec as P

D = 3584
smooth_width = 0.1
penalty = 0.0001
tiny_term = 1e-06
LAT = ("x", "zl")
TOK = ("y", "zh")
BF = jnp.bfloat16
F32 = jnp.float32
VMEM = pl.BlockSpec(memory_space=pltpu.VMEM)
SMEM = pl.BlockSpec(memory_space=pltpu.SMEM)
NT = (((1,), (1,)), ((), ()))


def swap(value, axis):
    return lax.ppermute(value, axis, [(0, 1), (1, 0)])


def gather(value, axes):
    size = lax.axis_size(axes)
    copies = jnp.broadcast_to(value[None], (size,) + value.shape)
    return lax.all_to_all(copies, axes, 0, 0, tiled=False)


def encode_kernel(at_ref, a_ref, enc_ref, keep_ref, send_ref, cols_ref, v_ref):
    pair_at, tok_at = at_ref[0], at_ref[2]
    v_ref[...] = jnp.dot(a_ref[...], enc_ref[...], preferred_element_type=F32)
    keep_ref[...] = v_ref[pl.ds(pl.multiple_of(pair_at * 128, 128), 128), :]
    send_ref[...] = v_ref[pl.ds(pl.multiple_of((1 - pair_at) * 128, 128), 128), :]
    base = (tok_at // 2) * 896 + (tok_at % 2) * 384
    window = a_ref[:, pl.ds(pl.multiple_of(base, 128), 512)]
    cols_ref[...] = jnp.where(tok_at % 2 == 1, window[:, 64:512], window[:, 0:448])


def decode_kernel(
    at_ref, g1, g2, p1, p2, dec_ref, out_ref, f_ref, nsq_ref, wide_ref, norm_ref
):
    pair_at, zh_at = at_ref[0], at_ref[1]

    nsq = jnp.zeros((8, 256), F32)
    for y in range(4):
        rows = g1[y, 384:400, :].astype(F32)
        nsq = nsq + (rows[0:8] + rows[8:16])
    nsq_ref[...] = nsq
    norm = jnp.sqrt(nsq) * 0.125
    high = norm.astype(BF).astype(F32)
    wide_ref[...] = jnp.zeros_like(wide_ref)
    for k in range(8):
        wide_ref[0:1, k * 256 : (k + 1) * 256] = high[k : k + 1]
        wide_ref[1:2, k * 256 : (k + 1) * 256] = (norm - high)[k : k + 1]
    norm_ref[...] = wide_ref[...].astype(BF)

    def place(half, own, oth):
        near = pl.multiple_of(half * 256 + zh_at * 128, 128)
        far = pl.multiple_of(half * 256 + (1 - zh_at) * 128, 128)
        for y in range(4):
            mine = pl.multiple_of((2 * y + zh_at) * 256, 256)
            theirs = pl.multiple_of((2 * y + 1 - zh_at) * 256, 256)
            f_ref[pl.ds(near, 128), pl.ds(mine, 256)] = own[y, 0:128, :]
            f_ref[pl.ds(far, 128), pl.ds(theirs, 256)] = own[y, 128:256, :]
            f_ref[pl.ds(far, 128), pl.ds(mine, 256)] = own[y, 256:384, :]
            f_ref[pl.ds(near, 128), pl.ds(theirs, 256)] = oth[y]

    place(pair_at, g1, g2)
    place(1 - pair_at, p1, p2)
    for half in range(2):
        feats = f_ref[half * 256 : (half + 1) * 256, :]
        value = lax.dot_general(feats, dec_ref[...], NT, preferred_element_type=F32)
        sparse = lax.dot_general(feats, norm_ref[...], NT, preferred_element_type=F32)
        value, sparse = value.astype(BF), sparse.astype(BF)
        for zh in range(2):
            for yy in range(2):
                src = (zh * 2 + yy) * 64
                dst = ((half * 2 + yy) * 2 + zh) * 64
                out_ref[dst : dst + 64, 0:448] = value[src : src + 64, :]
                out_ref[dst : dst + 64, 448:512] = sparse[src : src + 64, :]


def numer_kernel(at_ref, f_ref, near_ref, far_ref, dec_ref, num_ref, msq_ref, a_ref):
    zh_at, tok_at = at_ref[1], at_ref[2]
    for half in range(2):
        near = pl.multiple_of(half * 256 + zh_at * 128, 128)
        far = pl.multiple_of(half * 256 + (1 - zh_at) * 128, 128)
        a_ref[pl.ds(near, 128), :] = near_ref[half * 128 : (half + 1) * 128, :]
        a_ref[pl.ds(far, 128), :] = far_ref[half * 128 : (half + 1) * 128, :]
    for k in range(8):
        cols = slice(k * 256, (k + 1) * 256)
        inner = jnp.dot(a_ref[...], dec_ref[:, cols], preferred_element_type=F32)
        num_ref[k : k + 1, :] = jnp.sum(
            inner * f_ref[:, cols].astype(F32), axis=0, keepdims=True
        )
    own = f_ref[:, pl.ds(pl.multiple_of(tok_at * 256, 256), 256)].astype(F32)
    msq_ref[...] = jnp.sum(own * own, axis=0, keepdims=True)


def call(kernel, name, flops, outs, count, scratch):
    return pl.pallas_call(
        kernel,
        out_shape=tuple(jax.ShapeDtypeStruct(shape, kind) for shape, kind in outs),
        in_specs=[SMEM] + [VMEM] * count,
        out_specs=(VMEM,) * len(outs),
        scratch_shapes=[pltpu.VMEM(shape, kind) for shape, kind in scratch],
        compiler_params=pltpu.CompilerParams(vmem_limit_bytes=40 << 20),
        cost_estimate=pl.CostEstimate(
            flops=flops, bytes_accessed=6 << 20, transcendentals=0
        ),
        name=name,
    )


def body(activations, enc_weight, enc_bias, thresholds, dec_weight, dec_bias):
    pair_at = lax.axis_index("pair")
    x_at = lax.axis_index("x")
    zh_at = lax.axis_index("zh")
    tok_at = lax.axis_index(TOK)
    lat_at = lax.axis_index(LAT)
    act = activations[0]
    enc = enc_weight[0]
    dec = dec_weight[0]
    dec_t = dec.T
    own, width = enc.shape[1], dec.shape[1]
    tokens = 8 * act.shape[0]
    rows = tokens // lax.axis_size(LAT)
    at = jnp.stack([pair_at, zh_at, tok_at]).astype(jnp.int32)

    quarter = swap(lax.dynamic_slice_in_dim(act, x_at * 16, 16, 0), "zh")
    near = gather(act, "y").reshape(256, D)
    far = gather(quarter, ("y", "x")).reshape(256, D)

    dec_wide = dec.astype(F32)
    nsq_part = jnp.sum(dec_wide * dec_wide, axis=1).reshape(8, own)

    def split(value):
        high = value.astype(BF)
        return [high, (value - high.astype(F32)).astype(BF)]

    thresh_level = thresholds.astype(F32) * 0.25

    def features(keep, send):
        pre = keep + swap(send, "pair") + enc_bias
        return (pre * jax.nn.sigmoid((pre - thresh_level) / smooth_width)).astype(BF)

    enc_outs = [((128, own), F32), ((128, own), F32), ((256, width), BF)]
    enc_flops = 2 * 256 * D * own
    half_value = ((256, own), F32)
    encode = call(encode_kernel, "encode", enc_flops, enc_outs, 2, [half_value])
    keep, send, near_cols = encode(at, near, enc)
    feats_near = features(keep, send)
    over = swap(jnp.concatenate([feats_near] + split(nsq_part), axis=0), "zh")
    over_near = over[:128]
    nsq_both = nsq_part + over[128:136].astype(F32) + over[136:144].astype(F32)

    keep, send, far_cols = encode(at, far, enc)
    feats_far = features(keep, send)
    over_far = swap(feats_far, "zh")
    g1 = gather(
        jnp.concatenate([feats_near, over_near, feats_far] + split(nsq_both), axis=0), "y"
    )
    p1 = swap(g1, "pair")
    over_far, g1 = lax.optimization_barrier((over_far, g1))
    g2 = gather(over_far, "y")
    p2 = swap(g2, "pair")

    payload, block_feats, nsq_all = call(
        decode_kernel,
        "decode",
        2 * tokens * 8 * own * 512,
        [((tokens, 512), BF), ((tokens, 8 * own), BF), ((8, own), F32)],
        5,
        [((64, 8 * own), F32), ((64, 8 * own), BF)],
    )(at, g1, g2, p1, p2, dec_t)
    nsq_own = lax.dynamic_index_in_dim(nsq_all, tok_at, 0, keepdims=False)
    arrived = lax.all_to_all(payload, LAT, 0, 0, tiled=True)

    num_part, sum_sq = call(
        numer_kernel,
        "numer",
        2 * tokens * 8 * own * width,
        [((8, own), F32), ((1, own), F32)],
        4,
        [((tokens, width), BF)],
    )(at, block_feats, near_cols, far_cols, dec_t)
    mean_sq = sum_sq[0] / tokens

    total = jnp.sum(arrived.reshape(32, rows, 512).astype(F32), axis=0)
    recon_vals = total[:, :width] + dec_bias[0]
    sparse = total[:, width] + total[:, width + 1]
    own_row = (lat_at // 8) * 64 + (lat_at % 4) * rows
    act_own = jnp.where(
        (lat_at // 4) % 2 == zh_at,
        lax.dynamic_slice_in_dim(near_cols, own_row, rows, 0),
        lax.dynamic_slice_in_dim(far_cols, own_row, rows, 0),
    )
    residue = act_own.astype(F32) - recon_vals
    own_terms = jnp.sum(residue * residue, axis=1) / (2.0 * D) + penalty * sparse

    last = jnp.concatenate(
        [
            jnp.broadcast_to(num_part.reshape(1, 8, own), (2, 8, own)),
            jnp.broadcast_to(own_terms, (2, 8, rows)),
        ],
        axis=2,
    ).reshape(16, own + rows)
    got = lax.all_to_all(last, ("pair",) + TOK, 0, 0, tiled=True)
    token_loss = jnp.sum(got[:, own:], axis=0)
    mine = lax.dynamic_slice_in_dim(got, pair_at * 8, 8, 0)[:, :own]
    num_own = jnp.sum(mine, axis=0) / tokens
    scaling = num_own / (nsq_own * mean_sq + tiny_term)
    return (recon_vals.astype(BF)[None], token_loss, scaling[None])


def solution(mesh):
    fine = Mesh(mesh.devices.reshape(2, 4, 8, 4, 2), ("pair", "x", "zl", "y", "zh"))
    return jax.shard_map(
        body,
        mesh=fine,
        in_specs=(
            P("pair", TOK, None),
            P("pair", None, LAT + TOK),
            P(LAT + TOK),
            P(LAT + TOK),
            P("pair", LAT, TOK),
            P("pair", TOK),
        ),
        out_specs=(P("pair", LAT, TOK), P(LAT), P("pair", LAT + TOK)),
        check_vma=False,
    )
```

```python
import jax
import jax.numpy as jnp
from jax import lax
from jax.experimental import pallas as pl
from jax.experimental.pallas import tpu as pltpu
from jax.sharding import Mesh, PartitionSpec as P

D = 3584
smooth_width = 0.1
penalty = 0.0001
tiny_term = 1e-06
LAT = ("x", "zl")
TOK = ("y", "zh")
BF = jnp.bfloat16
F32 = jnp.float32
VMEM = pl.BlockSpec(memory_space=pltpu.VMEM)
HBM = pl.BlockSpec(memory_space=pltpu.HBM)
SMEM = pl.BlockSpec(memory_space=pltpu.SMEM)
NT = (((1,), (1,)), ((), ()))


def swap(value, axis):
    return lax.ppermute(value, axis, [(0, 1), (1, 0)])


def gather(value, axes):
    size = lax.axis_size(axes)
    copies = jnp.broadcast_to(value[None], (size,) + value.shape)
    return lax.all_to_all(copies, axes, 0, 0, tiled=False)


def encode_kernel(at_ref, b0, b1, b2, b3, far_ref, enc_ref, keep_ref, send_ref, a_ref, v_ref):
    step = pl.program_id(0)
    pair_at, zh_at, y_at = at_ref[0], at_ref[1], at_ref[3]

    @pl.when(step == 0)
    def _():
        v_ref[...] = jnp.zeros_like(v_ref)

    for ref, far in ((b0, 0), (b1, 3), (b2, 1), (b3, 2)):
        row = pl.multiple_of(zh_at * 256 + ((y_at + far) % 4) * 64, 64)
        a_ref[pl.ds(row, 64), :] = ref[...]
    a_ref[pl.ds(pl.multiple_of((1 - zh_at) * 256, 256), 256), :] = far_ref[...]
    v_ref[...] += jnp.dot(a_ref[...], enc_ref[...], preferred_element_type=F32)

    @pl.when(step == pl.num_programs(0) - 1)
    def _():
        for half in range(2):
            kept = pl.multiple_of(half * 256 + pair_at * 128, 128)
            sent = pl.multiple_of(half * 256 + (1 - pair_at) * 128, 128)
            keep_ref[half * 128 : (half + 1) * 128, :] = v_ref[pl.ds(kept, 128), :]
            send_ref[half * 128 : (half + 1) * 128, :] = v_ref[pl.ds(sent, 128), :]


def decode_kernel(
    at_ref,
    g1,
    g2,
    p1,
    p2,
    dec_hbm,
    out_hbm,
    f_hbm,
    nsq_ref,
    out_ref,
    f_ref,
    dec_ref,
    part_ref,
    wide_ref,
    norm_ref,
    sems,
):
    pair_at, zh_at = at_ref[0], at_ref[1]
    parts = [
        pltpu.make_async_copy(ref.at[:, pl.ds(256, 16)], part_ref.at[k], sems.at[k])
        for k, ref in enumerate((g1, g2))
    ]
    loads = [pltpu.make_async_copy(dec_hbm, dec_ref, sems.at[2])]
    for half, own, oth in ((pair_at, g1, g2), (1 - pair_at, p1, p2)):
        row = pl.ds(pl.multiple_of(half * 256, 256), 256)
        for y in range(4):
            for ref, zh in ((own, zh_at), (oth, 1 - zh_at)):
                col = pl.ds(pl.multiple_of((2 * y + zh) * 256, 256), 256)
                loads.append(
                    pltpu.make_async_copy(
                        ref.at[y, pl.ds(0, 256)], f_ref.at[row, col], sems.at[2 + len(loads)]
                    )
                )
    for copy in parts + loads:
        copy.start()

    for copy in parts:
        copy.wait()
    nsq = jnp.zeros((8, 256), F32)
    for k in range(2):
        for y in range(4):
            rows = part_ref[k, y].astype(F32)
            nsq = nsq + (rows[0:8] + rows[8:16])
    nsq_ref[...] = nsq
    norm = jnp.sqrt(nsq) * 0.125
    high = norm.astype(BF).astype(F32)
    wide_ref[...] = jnp.zeros_like(wide_ref)
    for k in range(8):
        wide_ref[0:1, k * 256 : (k + 1) * 256] = high[k : k + 1]
        wide_ref[1:2, k * 256 : (k + 1) * 256] = (norm - high)[k : k + 1]
    norm_ref[...] = wide_ref[...].astype(BF)

    for copy in loads:
        copy.wait()
    feats_out = pltpu.make_async_copy(f_ref, f_hbm, sems.at[19])
    feats_out.start()
    copies = []
    for half in range(2):
        feats = f_ref[half * 256 : (half + 1) * 256, :]
        value = lax.dot_general(feats, dec_ref[...], NT, preferred_element_type=F32)
        sparse = lax.dot_general(feats, norm_ref[...], NT, preferred_element_type=F32)
        value, sparse = value.astype(BF), sparse.astype(BF)
        for zh in range(2):
            for yy in range(2):
                src = (zh * 2 + yy) * 64
                dst = ((half * 2 + yy) * 2 + zh) * 64
                out_ref[dst : dst + 64, 0:448] = value[src : src + 64, :]
                out_ref[dst : dst + 64, 448:512] = sparse[src : src + 64, :]
        rows = pl.ds(half * 256, 256)
        copies.append(
            pltpu.make_async_copy(out_ref.at[rows], out_hbm.at[rows], sems.at[20 + half])
        )
        copies[half].start()
    for copy in copies:
        copy.wait()
    feats_out.wait()


def numer_kernel(
    at_ref, b0, b1, b2, b3, far_ref, f_ref, dec_ref, num_ref, msq_ref, own_ref, a_ref
):
    zh_at, tok_at, y_at, lat_at = at_ref[1], at_ref[2], at_ref[3], at_ref[4]
    base = pl.multiple_of((tok_at // 2) * 896 + (tok_at % 2) * 384, 128)

    def take(ref, row, y, zh):
        window = ref[pl.ds(row, 64), pl.ds(base, 512)]
        cols = jnp.where(tok_at % 2 == 1, window[:, 64:512], window[:, 0:448])
        at = (y // 2) * 256 + zh * 128 + (y % 2) * 64
        a_ref[pl.ds(pl.multiple_of(at, 64), 64), :] = cols

    for ref, far in ((b0, 0), (b1, 3), (b2, 1), (b3, 2)):
        take(ref, 0, (y_at + far) % 4, zh_at)
    for y in range(4):
        take(far_ref, y * 64, y, 1 - zh_at)
    own_y, own_zh = lat_at // 8, (lat_at // 4) % 2
    own_at = (own_y // 2) * 256 + own_zh * 128 + (own_y % 2) * 64 + (lat_at % 4) * 16
    own_ref[...] = a_ref[pl.ds(pl.multiple_of(own_at, 16), 16), :]
    for k in range(8):
        cols = slice(k * 256, (k + 1) * 256)
        inner = jnp.dot(a_ref[...], dec_ref[:, cols], preferred_element_type=F32)
        num_ref[k : k + 1, :] = jnp.sum(
            inner * f_ref[:, cols].astype(F32), axis=0, keepdims=True
        )
    feats = f_ref[:, pl.ds(pl.multiple_of(tok_at * 256, 256), 256)].astype(F32)
    msq_ref[...] = jnp.sum(feats * feats, axis=0, keepdims=True)


def call(kernel, name, flops, outs, count, scratch, outside=0, spaces=None):
    return pl.pallas_call(
        kernel,
        out_shape=tuple(jax.ShapeDtypeStruct(shape, kind) for shape, kind in outs),
        in_specs=[SMEM] + [VMEM] * count + [HBM] * outside,
        out_specs=spaces or (VMEM,) * len(outs),
        scratch_shapes=scratch,
        compiler_params=pltpu.CompilerParams(vmem_limit_bytes=60 << 20),
        cost_estimate=pl.CostEstimate(
            flops=flops, bytes_accessed=6 << 20, transcendentals=0
        ),
        name=name,
    )


def body(activations, enc_weight, enc_bias, thresholds, dec_weight, dec_bias):
    pair_at = lax.axis_index("pair")
    x_at = lax.axis_index("x")
    zh_at = lax.axis_index("zh")
    tok_at = lax.axis_index(TOK)
    lat_at = lax.axis_index(LAT)
    act = activations[0]
    enc = enc_weight[0]
    dec = dec_weight[0]
    dec_t = dec.T
    own, width = enc.shape[1], dec.shape[1]
    tokens = 8 * act.shape[0]
    rows = tokens // lax.axis_size(LAT)
    y_at = lax.axis_index("y")
    at = jnp.stack([pair_at, zh_at, tok_at, y_at, lat_at]).astype(jnp.int32)

    quarter = swap(lax.dynamic_slice_in_dim(act, x_at * 16, 16, 0), "zh")
    blocks = [act] + [
        lax.ppermute(act, "y", [(i, (i + k) % 4) for i in range(4)]) for k in (1, 3, 2)
    ]
    copies = jnp.broadcast_to(quarter[None], (16, 16, D))
    copies, blocks[1], blocks[2] = lax.optimization_barrier((copies, blocks[1], blocks[2]))
    far = lax.all_to_all(copies, ("y", "x"), 0, 0).reshape(256, D)

    dec_wide = dec.astype(F32)
    nsq_part = jnp.sum(dec_wide * dec_wide, axis=1).reshape(8, own)

    def split(value):
        high = value.astype(BF)
        return [high, (value - high.astype(F32)).astype(BF)]

    thresh_level = thresholds.astype(F32) * 0.25

    def pick(rows, cols, at_k):
        return pl.BlockSpec((rows, cols), at_k)

    chunk = 512
    along = [pick(64, chunk, lambda k: (0, k))] * 4 + [
        pick(256, chunk, lambda k: (0, k)),
        pick(chunk, own, lambda k: (k, 0)),
    ]
    keep, send = pl.pallas_call(
        encode_kernel,
        grid=(D // chunk,),
        out_shape=(jax.ShapeDtypeStruct((256, own), F32),) * 2,
        in_specs=[SMEM] + along,
        out_specs=(pick(256, own, lambda k: (0, 0)),) * 2,
        scratch_shapes=[pltpu.VMEM((tokens, chunk), BF), pltpu.VMEM((tokens, own), F32)],
        compiler_params=pltpu.CompilerParams(vmem_limit_bytes=60 << 20),
        cost_estimate=pl.CostEstimate(
            flops=2 * tokens * D * own, bytes_accessed=6 << 20, transcendentals=0
        ),
        name="encode",
    )(at, *blocks, far, enc)
    pre = keep + swap(send, "pair") + enc_bias
    feats = (pre * jax.nn.sigmoid((pre - thresh_level) / smooth_width)).astype(BF)
    feats = jnp.concatenate([feats] + split(nsq_part), axis=0)
    over = swap(feats, "zh")
    g1 = gather(feats, "y")
    p1 = swap(g1, "pair")
    over, g1 = lax.optimization_barrier((over, g1))
    g2 = gather(over, "y")
    p2 = swap(g2, "pair")

    payload, block_feats, nsq_all = call(
        decode_kernel,
        "decode",
        2 * tokens * 8 * own * 512,
        [((tokens, 512), BF), ((tokens, 8 * own), BF), ((8, own), F32)],
        0,
        [
            pltpu.VMEM((tokens, 512), BF),
            pltpu.VMEM((tokens, 8 * own), BF),
            pltpu.VMEM((width, 8 * own), BF),
            pltpu.VMEM((2, 4, 16, own), BF),
            pltpu.VMEM((64, 8 * own), F32),
            pltpu.VMEM((64, 8 * own), BF),
            pltpu.SemaphoreType.DMA((22,)),
        ],
        5,
        (HBM, HBM, VMEM),
    )(at, g1, g2, p1, p2, dec_t)
    nsq_own = lax.dynamic_index_in_dim(nsq_all, tok_at, 0, keepdims=False)
    arrived = lax.all_to_all(payload, LAT, 0, 0, tiled=True)

    num_part, sum_sq, act_own = call(
        numer_kernel,
        "numer",
        2 * tokens * 8 * own * width,
        [((8, own), F32), ((1, own), F32), ((rows, width), BF)],
        7,
        [pltpu.VMEM((tokens, width), BF)],
    )(at, *blocks, far, block_feats, dec_t)
    mean_sq = sum_sq[0] / tokens

    total = jnp.sum(arrived.reshape(32, rows, 512).astype(F32), axis=0)
    recon_vals = total[:, :width] + dec_bias[0]
    sparse = total[:, width] + total[:, width + 1]
    residue = act_own.astype(F32) - recon_vals
    own_terms = jnp.sum(residue * residue, axis=1) / (2.0 * D) + penalty * sparse

    last = jnp.concatenate(
        [
            jnp.broadcast_to(num_part.reshape(1, 8, own), (2, 8, own)),
            jnp.broadcast_to(own_terms, (2, 8, rows)),
        ],
        axis=2,
    ).reshape(16, own + rows)
    got = lax.all_to_all(last, ("pair",) + TOK, 0, 0, tiled=True)
    token_loss = jnp.sum(got[:, own:], axis=0)
    mine = lax.dynamic_slice_in_dim(got, pair_at * 8, 8, 0)[:, :own]
    num_own = jnp.sum(mine, axis=0) / tokens
    scaling = num_own / (nsq_own * mean_sq + tiny_term)
    return (recon_vals.astype(BF)[None], token_loss, scaling[None])


def solution(mesh):
    fine = Mesh(mesh.devices.reshape(2, 4, 8, 4, 2), ("pair", "x", "zl", "y", "zh"))
    return jax.shard_map(
        body,
        mesh=fine,
        in_specs=(
            P("pair", TOK, None),
            P("pair", None, LAT + TOK),
            P(LAT + TOK),
            P(LAT + TOK),
            P("pair", LAT, TOK),
            P("pair", TOK),
        ),
        out_specs=(P("pair", LAT, TOK), P(LAT), P("pair", LAT + TOK)),
        check_vma=False,
    )
```

```python
import jax
import jax.numpy as jnp
from jax import lax
from jax.experimental import pallas as pl
from jax.experimental.pallas import tpu as pltpu
from jax.sharding import Mesh, PartitionSpec as P

D = 3584
smooth_width = 0.1
penalty = 0.0001
tiny_term = 1e-06
LAT = ("x", "zl")
TOK = ("y", "zh")
BF = jnp.bfloat16
F32 = jnp.float32
VMEM = pl.BlockSpec(memory_space=pltpu.VMEM)
ANY = pl.BlockSpec(memory_space=pl.ANY)
SMEM = pl.BlockSpec(memory_space=pltpu.SMEM)
NT = (((1,), (1,)), ((), ()))


def swap(value, axis):
    return lax.ppermute(value, axis, [(0, 1), (1, 0)])


def gather(value, axes):
    size = lax.axis_size(axes)
    copies = jnp.broadcast_to(value[None], (size,) + value.shape)
    return lax.all_to_all(copies, axes, 0, 0, tiled=False)


def encode_kernel(at_ref, act_hbm, enc_hbm, keep_ref, send_ref, a_ref, enc_ref, v_ref, sems):
    pair_at = at_ref[0]
    count = a_ref.shape[0]
    chunk = a_ref.shape[2]
    loads = []
    for k in range(count):
        span = pl.ds(k * chunk, chunk)
        loads.append(
            (
                pltpu.make_async_copy(act_hbm.at[:, span], a_ref.at[k], sems.at[2 * k]),
                pltpu.make_async_copy(enc_hbm.at[span], enc_ref.at[k], sems.at[2 * k + 1]),
            )
        )
    for pair in loads:
        for copy in pair:
            copy.start()
    for k in range(count):
        for copy in loads[k]:
            copy.wait()
        part = jnp.dot(a_ref[k], enc_ref[k], preferred_element_type=F32)
        if k == 0:
            v_ref[...] = part
        else:
            v_ref[...] += part
    keep_ref[...] = v_ref[pl.ds(pl.multiple_of(pair_at * 128, 128), 128), :]
    send_ref[...] = v_ref[pl.ds(pl.multiple_of((1 - pair_at) * 128, 128), 128), :]


def decode_kernel(
    at_ref, g1, g2, p1, p2, dec_ref, out_ref, nsq_ref, f_ref, wide_ref, norm_ref
):
    pair_at, zh_at = at_ref[0], at_ref[1]

    nsq = jnp.zeros((8, 256), F32)
    for y in range(4):
        rows = g1[y, 384:400, :].astype(F32)
        nsq = nsq + (rows[0:8] + rows[8:16])
    nsq_ref[...] = nsq
    norm = jnp.sqrt(nsq) * 0.125
    high = norm.astype(BF).astype(F32)
    wide_ref[...] = jnp.zeros_like(wide_ref)
    for k in range(8):
        wide_ref[0:1, k * 256 : (k + 1) * 256] = high[k : k + 1]
        wide_ref[1:2, k * 256 : (k + 1) * 256] = (norm - high)[k : k + 1]
    norm_ref[...] = wide_ref[...].astype(BF)

    def place(half, own, oth):
        near = pl.multiple_of(half * 256 + zh_at * 128, 128)
        far = pl.multiple_of(half * 256 + (1 - zh_at) * 128, 128)
        for y in range(4):
            mine = pl.multiple_of((2 * y + zh_at) * 256, 256)
            theirs = pl.multiple_of((2 * y + 1 - zh_at) * 256, 256)
            f_ref[pl.ds(near, 128), pl.ds(mine, 256)] = own[y, 0:128, :]
            f_ref[pl.ds(far, 128), pl.ds(theirs, 256)] = own[y, 128:256, :]
            f_ref[pl.ds(far, 128), pl.ds(mine, 256)] = own[y, 256:384, :]
            f_ref[pl.ds(near, 128), pl.ds(theirs, 256)] = oth[y]

    place(pair_at, g1, g2)
    place(1 - pair_at, p1, p2)
    for half in range(2):
        feats = f_ref[half * 256 : (half + 1) * 256, :]
        value = lax.dot_general(feats, dec_ref[...], NT, preferred_element_type=F32)
        sparse = lax.dot_general(feats, norm_ref[...], NT, preferred_element_type=F32)
        value, sparse = value.astype(BF), sparse.astype(BF)
        for zh in range(2):
            for yy in range(2):
                src = (zh * 2 + yy) * 64
                dst = ((half * 2 + yy) * 2 + zh) * 64
                out_ref[dst : dst + 64, 0:448] = value[src : src + 64, :]
                out_ref[dst : dst + 64, 448:512] = sparse[src : src + 64, :]


def numer_kernel(
    at_ref,
    g1,
    g2,
    p1,
    p2,
    dec_ref,
    near_hbm,
    far_hbm,
    num_ref,
    msq_ref,
    own_ref,
    w_ref,
    a_ref,
    sems,
):
    pair_at, zh_at, tok_at, y_at, lat_at = [at_ref[k] for k in range(5)]
    base = pl.multiple_of((tok_at // 2) * 896 + (tok_at % 2) * 384, 128)
    loads = [
        pltpu.make_async_copy(ref.at[:, pl.ds(base, 512)], w_ref.at[k], sems.at[k])
        for k, ref in enumerate((near_hbm, far_hbm))
    ]
    for copy in loads:
        copy.start()
    for copy in loads:
        copy.wait()
    for k in range(2):
        for half in range(2):
            window = w_ref[k, half * 128 : (half + 1) * 128, :]
            cols = jnp.where(tok_at % 2 == 1, window[:, 64:512], window[:, 0:448])
            a_ref[half, k * 128 : (k + 1) * 128, :] = cols

    for y in range(4):
        for zh in range(2):
            at = 2 * y + (zh_at if zh == 0 else 1 - zh_at)
            cols = dec_ref[:, pl.ds(pl.multiple_of(at * 256, 256), 256)]
            total = jnp.zeros((1, 256), F32)
            for half, own, oth in ((pair_at, g1, g2), (1 - pair_at, p1, p2)):
                inner = jnp.dot(a_ref[half], cols, preferred_element_type=F32)
                near = own[y, 0:128, :] if zh == 0 else oth[y]
                far = own[y, 256:384, :] if zh == 0 else own[y, 128:256, :]
                both = inner[0:128] * near.astype(F32) + inner[128:256] * far.astype(F32)
                total = total + jnp.sum(both, axis=0, keepdims=True)
            num_ref[pl.ds(at, 1), :] = total

    squares = jnp.zeros((128, 256), F32)
    for own in (g1, p1):
        for rows in (slice(0, 128), slice(256, 384)):
            feats = own[y_at, rows, :].astype(F32)
            squares = squares + feats * feats
    msq_ref[...] = jnp.sum(squares, axis=0, keepdims=True)
    own_y, own_zh = lat_at // 8, (lat_at // 4) % 2
    row = jnp.where(own_zh == zh_at, 0, 128) + (own_y % 2) * 64 + (lat_at % 4) * 16
    own_ref[...] = a_ref[own_y // 2, pl.ds(pl.multiple_of(row, 16), 16), :]


def call(kernel, name, flops, outs, count, scratch, outside=0, limit=60):
    return pl.pallas_call(
        kernel,
        out_shape=tuple(jax.ShapeDtypeStruct(shape, kind) for shape, kind in outs),
        in_specs=[SMEM] + [VMEM] * count + [ANY] * outside,
        out_specs=(VMEM,) * len(outs),
        scratch_shapes=scratch,
        compiler_params=pltpu.CompilerParams(vmem_limit_bytes=limit << 20),
        cost_estimate=pl.CostEstimate(
            flops=flops, bytes_accessed=6 << 20, transcendentals=0
        ),
        name=name,
    )


def body(activations, enc_weight, enc_bias, thresholds, dec_weight, dec_bias):
    pair_at = lax.axis_index("pair")
    x_at = lax.axis_index("x")
    zh_at = lax.axis_index("zh")
    tok_at = lax.axis_index(TOK)
    lat_at = lax.axis_index(LAT)
    act = activations[0]
    enc = enc_weight[0]
    dec = dec_weight[0]
    dec_t = dec.T
    own, width = enc.shape[1], dec.shape[1]
    tokens = 8 * act.shape[0]
    rows = tokens // lax.axis_size(LAT)
    at = jnp.stack([pair_at, zh_at, tok_at, lax.axis_index("y"), lat_at]).astype(jnp.int32)

    quarter = swap(lax.dynamic_slice_in_dim(act, x_at * 16, 16, 0), "zh")
    near = gather(act, "y").reshape(256, D)
    far = gather(quarter, ("y", "x")).reshape(256, D)

    dec_wide = dec.astype(F32)
    nsq_part = jnp.sum(dec_wide * dec_wide, axis=1).reshape(8, own)

    def split(value):
        high = value.astype(BF)
        return [high, (value - high.astype(F32)).astype(BF)]

    thresh_level = thresholds.astype(F32) * 0.25

    def features(keep, send):
        pre = keep + swap(send, "pair") + enc_bias
        return (pre * jax.nn.sigmoid((pre - thresh_level) / smooth_width)).astype(BF)

    parts, chunk = 4, D // 4
    encode = call(
        encode_kernel,
        "encode",
        2 * 256 * D * own,
        [((128, own), F32), ((128, own), F32)],
        0,
        [
            pltpu.VMEM((parts, 256, chunk), BF),
            pltpu.VMEM((parts, chunk, own), BF),
            pltpu.VMEM((256, own), F32),
            pltpu.SemaphoreType.DMA((2 * parts,)),
        ],
        2,
    )
    keep, send = encode(at, near, enc)
    feats_near = features(keep, send)
    over = swap(jnp.concatenate([feats_near] + split(nsq_part), axis=0), "zh")
    over_near = over[:128]
    nsq_both = nsq_part + over[128:136].astype(F32) + over[136:144].astype(F32)

    keep, send = encode(at, far, enc)
    feats_far = features(keep, send)
    over_far = swap(feats_far, "zh")
    g1 = gather(
        jnp.concatenate([feats_near, over_near, feats_far] + split(nsq_both), axis=0), "y"
    )
    over_far, g1 = lax.optimization_barrier((over_far, g1))
    g2 = gather(over_far, "y")
    p1 = swap(g1, "pair")
    p2 = swap(g2, "pair")

    payload, nsq_all = call(
        decode_kernel,
        "decode",
        2 * tokens * 8 * own * 512,
        [((tokens, 512), BF), ((8, own), F32)],
        5,
        [
            pltpu.VMEM((tokens, 8 * own), BF),
            pltpu.VMEM((64, 8 * own), F32),
            pltpu.VMEM((64, 8 * own), BF),
        ],
        limit=40,
    )(at, g1, g2, p1, p2, dec_t)
    nsq_own = lax.dynamic_index_in_dim(nsq_all, tok_at, 0, keepdims=False)
    arrived = lax.all_to_all(payload, LAT, 0, 0, tiled=True)

    num_part, sum_sq, act_own = call(
        numer_kernel,
        "numer",
        2 * tokens * 8 * own * width,
        [((8, own), F32), ((1, own), F32), ((rows, width), BF)],
        5,
        [
            pltpu.VMEM((2, 256, 512), BF),
            pltpu.VMEM((2, 256, width), BF),
            pltpu.SemaphoreType.DMA((2,)),
        ],
        2,
    )(at, g1, g2, p1, p2, dec_t, near, far)
    mean_sq = sum_sq[0] / tokens

    total = jnp.sum(arrived.reshape(32, rows, 512).astype(F32), axis=0)
    recon_vals = total[:, :width] + dec_bias[0]
    sparse = total[:, width] + total[:, width + 1]
    residue = act_own.astype(F32) - recon_vals
    own_terms = jnp.sum(residue * residue, axis=1) / (2.0 * D) + penalty * sparse

    last = jnp.concatenate(
        [
            jnp.broadcast_to(num_part.reshape(1, 8, own), (2, 8, own)),
            jnp.broadcast_to(own_terms, (2, 8, rows)),
        ],
        axis=2,
    ).reshape(16, own + rows)
    got = lax.all_to_all(last, ("pair",) + TOK, 0, 0, tiled=True)
    token_loss = jnp.sum(got[:, own:], axis=0)
    mine = lax.dynamic_slice_in_dim(got, pair_at * 8, 8, 0)[:, :own]
    num_own = jnp.sum(mine, axis=0) / tokens
    scaling = num_own / (nsq_own * mean_sq + tiny_term)
    return (recon_vals.astype(BF)[None], token_loss, scaling[None])


def solution(mesh):
    fine = Mesh(mesh.devices.reshape(2, 4, 8, 4, 2), ("pair", "x", "zl", "y", "zh"))
    return jax.shard_map(
        body,
        mesh=fine,
        in_specs=(
            P("pair", TOK, None),
            P("pair", None, LAT + TOK),
            P(LAT + TOK),
            P(LAT + TOK),
            P("pair", LAT, TOK),
            P("pair", TOK),
        ),
        out_specs=(P("pair", LAT, TOK), P(LAT), P("pair", LAT + TOK)),
        check_vma=False,
    )
```

```python
import jax
import jax.numpy as jnp
from jax import lax
from jax.experimental import pallas as pl
from jax.experimental.pallas import tpu as pltpu
from jax.sharding import Mesh, PartitionSpec as P

D = 3584
smooth_width = 0.1
penalty = 0.0001
tiny_term = 1e-06
LAT = ("x", "zl")
TOK = ("y", "zh")
BF = jnp.bfloat16
F32 = jnp.float32
VMEM = pl.BlockSpec(memory_space=pltpu.VMEM)
ANY = pl.BlockSpec(memory_space=pl.ANY)
SMEM = pl.BlockSpec(memory_space=pltpu.SMEM)
STEPS = (0, 3, 1, 2)
NT = (((1,), (1,)), ((), ()))


def swap(value, axis):
    return lax.ppermute(value, axis, [(0, 1), (1, 0)])


def gather(value, axes):
    size = lax.axis_size(axes)
    copies = jnp.broadcast_to(value[None], (size,) + value.shape)
    return lax.all_to_all(copies, axes, 0, 0, tiled=False)


def decode_kernel(
    at_ref, g1, g2, p1, p2, dec_ref, out_ref, nsq_ref, f_ref, wide_ref, norm_ref
):
    pair_at, zh_at, y_at = at_ref[0], at_ref[1], at_ref[3]

    nsq = jnp.zeros((8, 256), F32)
    for y in range(4):
        rows = g1[y, 384:400, :].astype(F32)
        nsq = nsq + (rows[0:8] + rows[8:16])
    nsq_ref[...] = nsq
    norm = jnp.sqrt(nsq) * 0.125
    high = norm.astype(BF).astype(F32)
    wide_ref[...] = jnp.zeros_like(wide_ref)
    for k in range(8):
        wide_ref[0:1, k * 256 : (k + 1) * 256] = high[k : k + 1]
        wide_ref[1:2, k * 256 : (k + 1) * 256] = (norm - high)[k : k + 1]
    norm_ref[...] = wide_ref[...].astype(BF)

    def place(half, own, oth):
        near = pl.multiple_of(half * 256 + zh_at * 128, 128)
        far = pl.multiple_of(half * 256 + (1 - zh_at) * 128, 128)
        for y in range(4):
            ring_y = (y_at + STEPS[y]) % 4
            mine = pl.multiple_of((2 * ring_y + zh_at) * 256, 256)
            theirs = pl.multiple_of((2 * ring_y + 1 - zh_at) * 256, 256)
            last = pl.multiple_of((2 * y + 1 - zh_at) * 256, 256)
            f_ref[pl.ds(near, 128), pl.ds(mine, 256)] = own[y, 0:128, :]
            f_ref[pl.ds(far, 128), pl.ds(theirs, 256)] = own[y, 128:256, :]
            f_ref[pl.ds(far, 128), pl.ds(mine, 256)] = own[y, 256:384, :]
            f_ref[pl.ds(near, 128), pl.ds(last, 256)] = oth[y]

    place(pair_at, g1, g2)
    place(1 - pair_at, p1, p2)
    for half in range(2):
        feats = f_ref[half * 256 : (half + 1) * 256, :]
        value = lax.dot_general(feats, dec_ref[...], NT, preferred_element_type=F32)
        sparse = lax.dot_general(feats, norm_ref[...], NT, preferred_element_type=F32)
        value, sparse = value.astype(BF), sparse.astype(BF)
        for zh in range(2):
            for yy in range(2):
                src = (zh * 2 + yy) * 64
                dst = ((half * 2 + yy) * 2 + zh) * 64
                out_ref[dst : dst + 64, 0:448] = value[src : src + 64, :]
                out_ref[dst : dst + 64, 448:512] = sparse[src : src + 64, :]


def numer_kernel(
    at_ref,
    g1,
    g2,
    p1,
    p2,
    dec_ref,
    near_hbm,
    far_hbm,
    num_ref,
    msq_ref,
    own_ref,
    w_ref,
    a_ref,
    sems,
):
    pair_at, zh_at, tok_at, y_at, lat_at = [at_ref[k] for k in range(5)]
    base = pl.multiple_of((tok_at // 2) * 896 + (tok_at % 2) * 384, 128)
    loads = [
        pltpu.make_async_copy(ref.at[:, pl.ds(base, 512)], w_ref.at[k], sems.at[k])
        for k, ref in enumerate((near_hbm, far_hbm))
    ]
    for copy in loads:
        copy.start()
    for copy in loads:
        copy.wait()
    for k in range(2):
        for half in range(2):
            window = w_ref[k, half * 128 : (half + 1) * 128, :]
            cols = jnp.where(tok_at % 2 == 1, window[:, 64:512], window[:, 0:448])
            a_ref[half, k * 128 : (k + 1) * 128, :] = cols

    for k in range(4):
        y = (y_at + STEPS[k]) % 4
        for zh in range(2):
            at = 2 * y + (zh_at if zh == 0 else 1 - zh_at)
            cols = dec_ref[:, pl.ds(pl.multiple_of(at * 256, 256), 256)]
            total = jnp.zeros((1, 256), F32)
            for half, own, oth in ((pair_at, g1, g2), (1 - pair_at, p1, p2)):
                inner = jnp.dot(a_ref[half], cols, preferred_element_type=F32)
                near = own[k, 0:128, :] if zh == 0 else oth[y]
                far = own[k, 256:384, :] if zh == 0 else own[k, 128:256, :]
                both = inner[0:128] * near.astype(F32) + inner[128:256] * far.astype(F32)
                total = total + jnp.sum(both, axis=0, keepdims=True)
            num_ref[pl.ds(at, 1), :] = total

    squares = jnp.zeros((128, 256), F32)
    for own in (g1, p1):
        for rows in (slice(0, 128), slice(256, 384)):
            feats = own[0, rows, :].astype(F32)
            squares = squares + feats * feats
    msq_ref[...] = jnp.sum(squares, axis=0, keepdims=True)
    own_y, own_zh = lat_at // 8, (lat_at // 4) % 2
    row = jnp.where(own_zh == zh_at, 0, 128) + (own_y % 2) * 64 + (lat_at % 4) * 16
    own_ref[...] = a_ref[own_y // 2, pl.ds(pl.multiple_of(row, 16), 16), :]


def close_kernel(arrived_ref, bias_ref, act_ref, num_ref, recon_ref, last_ref):
    total = arrived_ref[0].astype(F32)
    for k in range(1, 32):
        total = total + arrived_ref[k].astype(F32)
    recon = total[:, 0:448] + bias_ref[...]
    recon_ref[...] = recon.astype(BF)
    residue = act_ref[...].astype(F32) - recon
    sparse = total[:, 448:449] + total[:, 449:450]
    terms = jnp.sum(residue * residue, axis=1, keepdims=True) / (2.0 * D) + penalty * sparse
    row = lax.broadcasted_iota(jnp.int32, (16, 128), 0)
    lane = lax.broadcasted_iota(jnp.int32, (16, 128), 1)
    line = jnp.sum(jnp.where(row == lane, terms, 0.0), axis=0, keepdims=True)
    for k in range(8):
        for pair in range(2):
            at = pair * 8 + k
            last_ref[at, 0:1, :] = num_ref[k : k + 1, 0:128]
            last_ref[at, 1:2, :] = num_ref[k : k + 1, 128:256]
            last_ref[at, 2:3, :] = line
            last_ref[at, 3:4, :] = line


def call(kernel, name, flops, outs, count, scratch, outside=0, limit=60):
    return pl.pallas_call(
        kernel,
        out_shape=tuple(jax.ShapeDtypeStruct(shape, kind) for shape, kind in outs),
        in_specs=[SMEM] + [VMEM] * count + [ANY] * outside,
        out_specs=(VMEM,) * len(outs),
        scratch_shapes=scratch,
        compiler_params=pltpu.CompilerParams(vmem_limit_bytes=limit << 20),
        cost_estimate=pl.CostEstimate(
            flops=flops, bytes_accessed=6 << 20, transcendentals=0
        ),
        name=name,
    )


def body(activations, enc_weight, enc_bias, thresholds, dec_weight, dec_bias):
    pair_at = lax.axis_index("pair")
    x_at = lax.axis_index("x")
    zh_at = lax.axis_index("zh")
    tok_at = lax.axis_index(TOK)
    lat_at = lax.axis_index(LAT)
    act = activations[0]
    enc = enc_weight[0]
    dec = dec_weight[0]
    dec_t = dec.T
    own, width = enc.shape[1], dec.shape[1]
    tokens = 8 * act.shape[0]
    rows = tokens // lax.axis_size(LAT)
    at = jnp.stack([pair_at, zh_at, tok_at, lax.axis_index("y"), lat_at]).astype(jnp.int32)

    quarter = swap(lax.dynamic_slice_in_dim(act, x_at * 16, 16, 0), "zh")
    near = gather(act, "y").reshape(256, D)
    far = gather(quarter, ("y", "x")).reshape(256, D)

    dec_wide = dec.astype(F32)
    nsq_part = jnp.sum(dec_wide * dec_wide, axis=1).reshape(8, own)

    def split(value):
        high = value.astype(BF)
        return [high, (value - high.astype(F32)).astype(BF)]

    thresh_level = thresholds.astype(F32) * 0.25

    def features(acts):
        part = jnp.dot(acts, enc, preferred_element_type=F32)
        keep = lax.dynamic_slice_in_dim(part, pair_at * 128, 128, 0)
        send = lax.dynamic_slice_in_dim(part, (1 - pair_at) * 128, 128, 0)
        pre = keep + swap(send, "pair") + enc_bias
        return (pre * jax.nn.sigmoid((pre - thresh_level) / smooth_width)).astype(BF)

    feats_near = features(near)
    over = swap(jnp.concatenate([feats_near] + split(nsq_part), axis=0), "zh")
    over_near = over[:128]
    nsq_both = nsq_part + over[128:136].astype(F32) + over[136:144].astype(F32)

    feats_far = features(far)
    over_far = lax.dynamic_index_in_dim(gather(feats_far, "zh"), 1 - zh_at, 0, False)
    packed = jnp.concatenate([feats_near, over_near, feats_far] + split(nsq_both), axis=0)
    ring = [
        lax.ppermute(packed, "y", [(i, (i + k) % 4) for i in range(4)]) for k in (1, 3, 2)
    ]
    over_far, *ring = lax.optimization_barrier((over_far, *ring))
    g1 = jnp.stack([packed] + ring)
    g2 = gather(over_far, "y")
    p1 = swap(g1, "pair")
    p2 = swap(g2, "pair")

    payload, nsq_all = call(
        decode_kernel,
        "decode",
        2 * tokens * 8 * own * 512,
        [((tokens, 512), BF), ((8, own), F32)],
        5,
        [
            pltpu.VMEM((tokens, 8 * own), BF),
            pltpu.VMEM((64, 8 * own), F32),
            pltpu.VMEM((64, 8 * own), BF),
        ],
        limit=40,
    )(at, g1, g2, p1, p2, dec_t)
    nsq_own = lax.dynamic_index_in_dim(nsq_all, tok_at, 0, keepdims=False)
    arrived = lax.all_to_all(payload, LAT, 0, 0, tiled=True)

    num_part, sum_sq, act_own = call(
        numer_kernel,
        "numer",
        2 * tokens * 8 * own * width,
        [((8, own), F32), ((1, own), F32), ((rows, width), BF)],
        5,
        [
            pltpu.VMEM((2, 256, 512), BF),
            pltpu.VMEM((2, 256, width), BF),
            pltpu.SemaphoreType.DMA((2,)),
        ],
        2,
    )(at, g1, g2, p1, p2, dec_t, near, far)
    mean_sq = sum_sq[0] / tokens

    recon, last = pl.pallas_call(
        close_kernel,
        out_shape=(
            jax.ShapeDtypeStruct((rows, width), BF),
            jax.ShapeDtypeStruct((16, 4, 128), F32),
        ),
        in_specs=[VMEM] * 4,
        out_specs=(VMEM, VMEM),
        compiler_params=pltpu.CompilerParams(vmem_limit_bytes=16 << 20),
        cost_estimate=pl.CostEstimate(
            flops=1 << 20, bytes_accessed=1 << 20, transcendentals=0
        ),
        name="close",
    )(arrived.reshape(32, rows, 512), dec_bias, act_own, num_part)
    got = lax.all_to_all(last, ("pair",) + TOK, 0, 0, tiled=True)
    token_loss = jnp.sum(got[:, 2, :rows], axis=0)
    mine = lax.dynamic_slice_in_dim(got, pair_at * 8, 8, 0)[:, :2, :]
    num_own = jnp.sum(mine, axis=0).reshape(own) / tokens
    scaling = num_own / (nsq_own * mean_sq + tiny_term)
    return (recon[None], token_loss, scaling[None])


def solution(mesh):
    fine = Mesh(mesh.devices.reshape(2, 4, 8, 4, 2), ("pair", "x", "zl", "y", "zh"))
    return jax.shard_map(
        body,
        mesh=fine,
        in_specs=(
            P("pair", TOK, None),
            P("pair", None, LAT + TOK),
            P(LAT + TOK),
            P(LAT + TOK),
            P("pair", LAT, TOK),
            P("pair", TOK),
        ),
        out_specs=(P("pair", LAT, TOK), P(LAT), P("pair", LAT + TOK)),
        check_vma=False,
    )
```

```python
import jax
import jax.numpy as jnp
from jax import lax
from jax.experimental import pallas as pl
from jax.experimental.pallas import tpu as pltpu
from jax.sharding import Mesh, PartitionSpec as P

D = 3584
smooth_width = 0.1
penalty = 0.0001
tiny_term = 1e-06
LAT = ("x", "zl")
TOK = ("y", "zh")
BF = jnp.bfloat16
F32 = jnp.float32
VMEM = pl.BlockSpec(memory_space=pltpu.VMEM)
HBM = pl.BlockSpec(memory_space=pltpu.HBM)
SMEM = pl.BlockSpec(memory_space=pltpu.SMEM)
NT = (((1,), (1,)), ((), ()))


def swap(value, axis):
    return lax.ppermute(value, axis, [(0, 1), (1, 0)])


def gather(value, axes):
    size = lax.axis_size(axes)
    copies = jnp.broadcast_to(value[None], (size,) + value.shape)
    return lax.all_to_all(copies, axes, 0, 0, tiled=False)


def encode_kernel(at_ref, act_hbm, enc_hbm, keep_ref, send_ref, a_ref, enc_ref, v_ref, sems):
    pair_at = at_ref[0]
    count = a_ref.shape[0]
    chunk = a_ref.shape[2]
    loads = []
    for k in range(count):
        span = pl.ds(k * chunk, chunk)
        loads.append(
            (
                pltpu.make_async_copy(act_hbm.at[:, span], a_ref.at[k], sems.at[2 * k]),
                pltpu.make_async_copy(enc_hbm.at[span], enc_ref.at[k], sems.at[2 * k + 1]),
            )
        )
    for pair in loads:
        for copy in pair:
            copy.start()
    for k in range(count):
        for copy in loads[k]:
            copy.wait()
        part = jnp.dot(a_ref[k], enc_ref[k], preferred_element_type=F32)
        if k == 0:
            v_ref[...] = part
        else:
            v_ref[...] += part
    keep_ref[...] = v_ref[pl.ds(pl.multiple_of(pair_at * 128, 128), 128), :]
    send_ref[...] = v_ref[pl.ds(pl.multiple_of((1 - pair_at) * 128, 128), 128), :]


def decode_kernel(
    at_ref, g1, g2, p1, p2, dec_ref, out_ref, nsq_ref, f_ref, wide_ref, norm_ref
):
    pair_at, zh_at = at_ref[0], at_ref[1]

    nsq = jnp.zeros((8, 256), F32)
    for y in range(4):
        rows = g1[y, 384:400, :].astype(F32)
        nsq = nsq + (rows[0:8] + rows[8:16])
    nsq_ref[...] = nsq
    norm = jnp.sqrt(nsq) * 0.125
    high = norm.astype(BF).astype(F32)
    wide_ref[...] = jnp.zeros_like(wide_ref)
    for k in range(8):
        wide_ref[0:1, k * 256 : (k + 1) * 256] = high[k : k + 1]
        wide_ref[1:2, k * 256 : (k + 1) * 256] = (norm - high)[k : k + 1]
    norm_ref[...] = wide_ref[...].astype(BF)

    def place(half, own, oth):
        near = pl.multiple_of(half * 256 + zh_at * 128, 128)
        far = pl.multiple_of(half * 256 + (1 - zh_at) * 128, 128)
        for y in range(4):
            mine = pl.multiple_of((2 * y + zh_at) * 256, 256)
            theirs = pl.multiple_of((2 * y + 1 - zh_at) * 256, 256)
            f_ref[pl.ds(near, 128), pl.ds(mine, 256)] = own[y, 0:128, :]
            f_ref[pl.ds(far, 128), pl.ds(theirs, 256)] = own[y, 128:256, :]
            f_ref[pl.ds(far, 128), pl.ds(mine, 256)] = own[y, 256:384, :]
            f_ref[pl.ds(near, 128), pl.ds(theirs, 256)] = oth[y]

    place(pair_at, g1, g2)
    place(1 - pair_at, p1, p2)
    for half in range(2):
        feats = f_ref[half * 256 : (half + 1) * 256, :]
        value = lax.dot_general(feats, dec_ref[...], NT, preferred_element_type=F32)
        sparse = lax.dot_general(feats, norm_ref[...], NT, preferred_element_type=F32)
        value, sparse = value.astype(BF), sparse.astype(BF)
        for zh in range(2):
            for yy in range(2):
                src = (zh * 2 + yy) * 64
                dst = ((half * 2 + yy) * 2 + zh) * 64
                out_ref[dst : dst + 64, 0:448] = value[src : src + 64, :]
                out_ref[dst : dst + 64, 448:512] = sparse[src : src + 64, :]


def numer_kernel(
    at_ref,
    g1,
    g2,
    p1,
    p2,
    dec_ref,
    near_hbm,
    far_hbm,
    num_ref,
    msq_ref,
    own_ref,
    w_ref,
    a_ref,
    sems,
):
    pair_at, zh_at, tok_at, y_at, lat_at = [at_ref[k] for k in range(5)]
    base = pl.multiple_of((tok_at // 2) * 896 + (tok_at % 2) * 384, 128)
    loads = [
        pltpu.make_async_copy(ref.at[:, pl.ds(base, 512)], w_ref.at[k], sems.at[k])
        for k, ref in enumerate((near_hbm, far_hbm))
    ]
    for copy in loads:
        copy.start()
    for copy in loads:
        copy.wait()
    for k in range(2):
        for half in range(2):
            window = w_ref[k, half * 128 : (half + 1) * 128, :]
            cols = jnp.where(tok_at % 2 == 1, window[:, 64:512], window[:, 0:448])
            a_ref[half, k * 128 : (k + 1) * 128, :] = cols

    for y in range(4):
        for zh in range(2):
            at = 2 * y + (zh_at if zh == 0 else 1 - zh_at)
            cols = dec_ref[:, pl.ds(pl.multiple_of(at * 256, 256), 256)]
            total = jnp.zeros((1, 256), F32)
            for half, own, oth in ((pair_at, g1, g2), (1 - pair_at, p1, p2)):
                inner = jnp.dot(a_ref[half], cols, preferred_element_type=F32)
                near = own[y, 0:128, :] if zh == 0 else oth[y]
                far = own[y, 256:384, :] if zh == 0 else own[y, 128:256, :]
                both = inner[0:128] * near.astype(F32) + inner[128:256] * far.astype(F32)
                total = total + jnp.sum(both, axis=0, keepdims=True)
            num_ref[pl.ds(at, 1), :] = total

    squares = jnp.zeros((128, 256), F32)
    for own in (g1, p1):
        for rows in (slice(0, 128), slice(256, 384)):
            feats = own[y_at, rows, :].astype(F32)
            squares = squares + feats * feats
    msq_ref[...] = jnp.sum(squares, axis=0, keepdims=True)
    own_y, own_zh = lat_at // 8, (lat_at // 4) % 2
    row = jnp.where(own_zh == zh_at, 0, 128) + (own_y % 2) * 64 + (lat_at % 4) * 16
    own_ref[...] = a_ref[own_y // 2, pl.ds(pl.multiple_of(row, 16), 16), :]


def close_kernel(
    arrived_ref, bias_ref, act_hbm, num_hbm, recon_ref, last_ref, act_ref, num_ref, sems
):
    loads = [
        pltpu.make_async_copy(act_hbm, act_ref, sems.at[0]),
        pltpu.make_async_copy(num_hbm, num_ref, sems.at[1]),
    ]
    for copy in loads:
        copy.start()
    total = arrived_ref[0].astype(F32)
    for k in range(1, 32):
        total = total + arrived_ref[k].astype(F32)
    recon = total[:, 0:448] + bias_ref[...]
    recon_ref[...] = recon.astype(BF)
    for copy in loads:
        copy.wait()
    residue = act_ref[...].astype(F32) - recon
    sparse = total[:, 448:449] + total[:, 449:450]
    terms = jnp.sum(residue * residue, axis=1, keepdims=True) / (2.0 * D) + penalty * sparse
    row = lax.broadcasted_iota(jnp.int32, (16, 128), 0)
    lane = lax.broadcasted_iota(jnp.int32, (16, 128), 1)
    line = jnp.sum(jnp.where(row == lane, terms, 0.0), axis=0, keepdims=True)
    for k in range(8):
        for pair in range(2):
            at = pair * 8 + k
            last_ref[at, 0:1, :] = num_ref[k : k + 1, 0:128]
            last_ref[at, 1:2, :] = num_ref[k : k + 1, 128:256]
            last_ref[at, 2:3, :] = line
            last_ref[at, 3:4, :] = line


def call(kernel, name, flops, outs, count, scratch, outside=0, limit=60):
    return pl.pallas_call(
        kernel,
        out_shape=tuple(jax.ShapeDtypeStruct(shape, kind) for shape, kind in outs),
        in_specs=[SMEM] + [VMEM] * count + [HBM] * outside,
        out_specs=(VMEM,) * len(outs),
        scratch_shapes=scratch,
        compiler_params=pltpu.CompilerParams(vmem_limit_bytes=limit << 20),
        cost_estimate=pl.CostEstimate(
            flops=flops, bytes_accessed=6 << 20, transcendentals=0
        ),
        name=name,
    )


def body(activations, enc_weight, enc_bias, thresholds, dec_weight, dec_bias):
    pair_at = lax.axis_index("pair")
    x_at = lax.axis_index("x")
    zh_at = lax.axis_index("zh")
    tok_at = lax.axis_index(TOK)
    lat_at = lax.axis_index(LAT)
    act = activations[0]
    enc = enc_weight[0]
    dec = dec_weight[0]
    dec_t = dec.T
    own, width = enc.shape[1], dec.shape[1]
    tokens = 8 * act.shape[0]
    rows = tokens // lax.axis_size(LAT)
    at = jnp.stack([pair_at, zh_at, tok_at, lax.axis_index("y"), lat_at]).astype(jnp.int32)

    quarter = swap(lax.dynamic_slice_in_dim(act, x_at * 16, 16, 0), "zh")
    near = gather(act, "y").reshape(256, D)
    far = gather(quarter, ("y", "x")).reshape(256, D)

    dec_wide = dec.astype(F32)
    nsq_part = jnp.sum(dec_wide * dec_wide, axis=1).reshape(8, own)

    def split(value):
        high = value.astype(BF)
        return [high, (value - high.astype(F32)).astype(BF)]

    thresh_level = thresholds.astype(F32) * 0.25

    parts, chunk = 4, D // 4
    encode = call(
        encode_kernel,
        "encode",
        2 * 256 * D * own,
        [((128, own), F32), ((128, own), F32)],
        0,
        [
            pltpu.VMEM((parts, 256, chunk), BF),
            pltpu.VMEM((parts, chunk, own), BF),
            pltpu.VMEM((256, own), F32),
            pltpu.SemaphoreType.DMA((2 * parts,)),
        ],
        2,
    )
    def features(acts, ahead):
        if ahead:
            keep, send = encode(at, acts, enc)
        else:
            part = jnp.dot(acts, enc, preferred_element_type=F32)
            keep = lax.dynamic_slice_in_dim(part, pair_at * 128, 128, 0)
            send = lax.dynamic_slice_in_dim(part, (1 - pair_at) * 128, 128, 0)
        pre = keep + swap(send, "pair") + enc_bias
        return (pre * jax.nn.sigmoid((pre - thresh_level) / smooth_width)).astype(BF)

    feats_near = features(near, True)
    over = swap(jnp.concatenate([feats_near] + split(nsq_part), axis=0), "zh")
    over_near = over[:128]
    nsq_both = nsq_part + over[128:136].astype(F32) + over[136:144].astype(F32)

    feats_far = features(far, False)
    over_far = swap(feats_far, "zh")
    g1 = gather(
        jnp.concatenate([feats_near, over_near, feats_far] + split(nsq_both), axis=0), "y"
    )
    over_far, g1 = lax.optimization_barrier((over_far, g1))
    g2 = gather(over_far, "y")
    p1 = swap(g1, "pair")
    p2 = swap(g2, "pair")

    payload, nsq_all = call(
        decode_kernel,
        "decode",
        2 * tokens * 8 * own * 512,
        [((tokens, 512), BF), ((8, own), F32)],
        5,
        [
            pltpu.VMEM((tokens, 8 * own), BF),
            pltpu.VMEM((64, 8 * own), F32),
            pltpu.VMEM((64, 8 * own), BF),
        ],
        limit=40,
    )(at, g1, g2, p1, p2, dec_t)
    nsq_own = lax.dynamic_index_in_dim(nsq_all, tok_at, 0, keepdims=False)
    arrived = lax.all_to_all(payload, LAT, 0, 0, tiled=True)

    num_part, sum_sq, act_own = call(
        numer_kernel,
        "numer",
        2 * tokens * 8 * own * width,
        [((8, own), F32), ((1, own), F32), ((rows, width), BF)],
        5,
        [
            pltpu.VMEM((2, 256, 512), BF),
            pltpu.VMEM((2, 256, width), BF),
            pltpu.SemaphoreType.DMA((2,)),
        ],
        2,
        limit=40,
    )(at, g1, g2, p1, p2, dec_t, near, far)
    mean_sq = sum_sq[0] / tokens

    recon, last = pl.pallas_call(
        close_kernel,
        out_shape=(
            jax.ShapeDtypeStruct((rows, width), BF),
            jax.ShapeDtypeStruct((16, 4, 128), F32),
        ),
        in_specs=[VMEM, VMEM, HBM, HBM],
        out_specs=(VMEM, VMEM),
        scratch_shapes=[
            pltpu.VMEM((rows, width), BF),
            pltpu.VMEM((8, own), F32),
            pltpu.SemaphoreType.DMA((2,)),
        ],
        compiler_params=pltpu.CompilerParams(vmem_limit_bytes=16 << 20),
        cost_estimate=pl.CostEstimate(
            flops=1 << 20, bytes_accessed=1 << 20, transcendentals=0
        ),
        name="close",
    )(arrived.reshape(32, rows, 512), dec_bias, act_own, num_part)
    got = lax.all_to_all(last, ("pair",) + TOK, 0, 0, tiled=True)
    token_loss = jnp.sum(got[:, 2, :rows], axis=0)
    mine = lax.dynamic_slice_in_dim(got, pair_at * 8, 8, 0)[:, :2, :]
    num_own = jnp.sum(mine, axis=0).reshape(own) / tokens
    scaling = num_own / (nsq_own * mean_sq + tiny_term)
    return (recon[None], token_loss, scaling[None])


def solution(mesh):
    fine = Mesh(mesh.devices.reshape(2, 4, 8, 4, 2), ("pair", "x", "zl", "y", "zh"))
    return jax.shard_map(
        body,
        mesh=fine,
        in_specs=(
            P("pair", TOK, None),
            P("pair", None, LAT + TOK),
            P(LAT + TOK),
            P(LAT + TOK),
            P("pair", LAT, TOK),
            P("pair", TOK),
        ),
        out_specs=(P("pair", LAT, TOK), P(LAT), P("pair", LAT + TOK)),
        check_vma=False,
    )
```

```python
import jax
import jax.numpy as jnp
from jax import lax
from jax.experimental import pallas as pl
from jax.experimental.pallas import tpu as pltpu
from jax.sharding import Mesh, PartitionSpec as P

D = 3584
smooth_width = 0.1
penalty = 0.0001
tiny_term = 1e-06
LAT = ("x", "zl")
TOK = ("y", "zh")
BF = jnp.bfloat16
F32 = jnp.float32
VMEM = pl.BlockSpec(memory_space=pltpu.VMEM)
HBM = pl.BlockSpec(memory_space=pltpu.HBM)
SMEM = pl.BlockSpec(memory_space=pltpu.SMEM)
NT = (((1,), (1,)), ((), ()))


def swap(value, axis):
    return lax.ppermute(value, axis, [(0, 1), (1, 0)])


def gather(value, axes):
    size = lax.axis_size(axes)
    copies = jnp.broadcast_to(value[None], (size,) + value.shape)
    return lax.all_to_all(copies, axes, 0, 0, tiled=False)


def encode_kernel(at_ref, act_hbm, enc_hbm, keep_ref, send_ref, a_ref, enc_ref, v_ref, sems):
    pair_at = at_ref[0]
    count = a_ref.shape[0]
    chunk = a_ref.shape[2]
    loads = []
    for k in range(count):
        span = pl.ds(k * chunk, chunk)
        loads.append(
            (
                pltpu.make_async_copy(act_hbm.at[:, span], a_ref.at[k], sems.at[2 * k]),
                pltpu.make_async_copy(enc_hbm.at[span], enc_ref.at[k], sems.at[2 * k + 1]),
            )
        )
    for pair in loads:
        for copy in pair:
            copy.start()
    for k in range(count):
        for copy in loads[k]:
            copy.wait()
        part = jnp.dot(a_ref[k], enc_ref[k], preferred_element_type=F32)
        if k == 0:
            v_ref[...] = part
        else:
            v_ref[...] += part
    for j in range(16):
        rows = slice(j * 8, (j + 1) * 8)
        kept = pl.multiple_of(j * 16 + pair_at * 8, 8)
        sent = pl.multiple_of(j * 16 + (1 - pair_at) * 8, 8)
        keep_ref[rows, :] = v_ref[pl.ds(kept, 8), :]
        send_ref[rows, :] = v_ref[pl.ds(sent, 8), :]


def decode_kernel(
    at_ref, g1, g2, dec_ref, oth_ref, out_ref, nsq_ref, f_ref, wide_ref, norm_ref
):
    zh_at = at_ref[1]

    nsq = [jnp.zeros((8, 256), F32)] * 2
    for y in range(4):
        rows = g1[y, 384:416, :].astype(F32)
        nsq[0] = nsq[0] + (rows[0:8] + rows[8:16])
        nsq[1] = nsq[1] + (rows[16:24] + rows[24:32])
    nsq_ref[...] = nsq[0]
    norm = (jnp.sqrt(nsq[0]) + jnp.sqrt(nsq[1])) * 0.125
    high = norm.astype(BF).astype(F32)
    wide_ref[...] = jnp.zeros_like(wide_ref)
    for k in range(8):
        wide_ref[0:1, k * 256 : (k + 1) * 256] = high[k : k + 1]
        wide_ref[1:2, k * 256 : (k + 1) * 256] = (norm - high)[k : k + 1]
    norm_ref[...] = wide_ref[...].astype(BF)

    for y in range(4):
        mine = pl.multiple_of((2 * y + zh_at) * 256, 256)
        theirs = pl.multiple_of((2 * y + 1 - zh_at) * 256, 256)
        f_ref[0:128, pl.ds(mine, 256)] = g1[y, 0:128, :]
        f_ref[128:256, pl.ds(theirs, 256)] = g1[y, 128:256, :]
        f_ref[128:256, pl.ds(mine, 256)] = g1[y, 256:384, :]
        f_ref[0:128, pl.ds(theirs, 256)] = g2[y]
    feats = f_ref[...]
    out = []
    for ref in (dec_ref, norm_ref, oth_ref):
        value = lax.dot_general(feats, ref[...], NT, preferred_element_type=F32)
        out.append(value.astype(BF))
    for half in range(2):
        zh = zh_at if half == 0 else 1 - zh_at
        for y in range(4):
            src = slice(half * 128 + y * 32, half * 128 + (y + 1) * 32)
            dst = pl.ds(pl.multiple_of((2 * y + zh) * 32, 32), 32)
            out_ref[dst, 0:448] = out[0][src]
            out_ref[dst, 448:512] = out[1][src]
            out_ref[dst, 512:960] = out[2][src]
            out_ref[dst, 960:1024] = jnp.zeros((32, 64), BF)


def numer_kernel(
    at_ref, g1, g2, dec_ref, oth_ref, own_ref, his_ref, num_ref, his_num_ref, msq_ref
):
    zh_at, y_at = at_ref[1], at_ref[3]
    for acts, dec, num in ((own_ref, dec_ref, num_ref), (his_ref, oth_ref, his_num_ref)):
        for y in range(4):
            for zh in range(2):
                at = 2 * y + (zh_at if zh == 0 else 1 - zh_at)
                cols = dec[:, pl.ds(pl.multiple_of(at * 256, 256), 256)]
                inner = jnp.dot(acts[...], cols, preferred_element_type=F32)
                near = g1[y, 0:128, :] if zh == 0 else g2[y]
                far = g1[y, 256:384, :] if zh == 0 else g1[y, 128:256, :]
                both = inner[0:128] * near.astype(F32) + inner[128:256] * far.astype(F32)
                num[pl.ds(at, 1), :] = jnp.sum(both, axis=0, keepdims=True)

    squares = jnp.zeros((128, 256), F32)
    for rows in (slice(0, 128), slice(256, 384)):
        feats = g1[y_at, rows, :].astype(F32)
        squares = squares + feats * feats
    msq_ref[...] = jnp.sum(squares, axis=0, keepdims=True)


def close_kernel(
    at_ref,
    arrived_ref,
    bias_ref,
    his_bias_ref,
    act_ref,
    his_act_ref,
    num_ref,
    his_num_ref,
    recon_ref,
    his_recon_ref,
    last_ref,
):
    pair_at = at_ref[0]
    total = arrived_ref[0].astype(F32)
    for k in range(1, 32):
        total = total + arrived_ref[k].astype(F32)
    terms = penalty * (total[:, 448:449] + total[:, 449:450])
    for at, bias, act, out in (
        (0, bias_ref, act_ref, recon_ref),
        (512, his_bias_ref, his_act_ref, his_recon_ref),
    ):
        recon = total[:, at : at + 448] + bias[...]
        out[...] = recon.astype(BF)
        residue = act[...].astype(F32) - recon
        terms = terms + jnp.sum(residue * residue, axis=1, keepdims=True) / (2.0 * D)
    row = lax.broadcasted_iota(jnp.int32, (8, 128), 0)
    lane = lax.broadcasted_iota(jnp.int32, (8, 128), 1)
    line = jnp.sum(jnp.where(row + pair_at * 8 == lane, terms, 0.0), axis=0, keepdims=True)
    for pair in range(2):
        num = jnp.where(pair_at == pair, num_ref[...], his_num_ref[...])
        for k in range(8):
            at = pair * 8 + k
            last_ref[at, 0:1, :] = num[k : k + 1, 0:128]
            last_ref[at, 1:2, :] = num[k : k + 1, 128:256]
            last_ref[at, 2:3, :] = line
            last_ref[at, 3:4, :] = line


def call(kernel, name, flops, outs, count, scratch, outside=0, limit=60):
    return pl.pallas_call(
        kernel,
        out_shape=tuple(jax.ShapeDtypeStruct(shape, kind) for shape, kind in outs),
        in_specs=[SMEM] + [VMEM] * count + [HBM] * outside,
        out_specs=(VMEM,) * len(outs),
        scratch_shapes=scratch,
        compiler_params=pltpu.CompilerParams(vmem_limit_bytes=limit << 20),
        cost_estimate=pl.CostEstimate(
            flops=flops, bytes_accessed=6 << 20, transcendentals=0
        ),
        name=name,
    )


def body(activations, enc_weight, enc_bias, thresholds, dec_weight, dec_bias):
    pair_at = lax.axis_index("pair")
    x_at = lax.axis_index("x")
    zh_at = lax.axis_index("zh")
    tok_at = lax.axis_index(TOK)
    lat_at = lax.axis_index(LAT)
    act = activations[0]
    enc = enc_weight[0]
    dec = dec_weight[0]
    dec_t = dec.T
    own, width = enc.shape[1], dec.shape[1]
    tokens = 8 * act.shape[0]
    rows = tokens // lax.axis_size(LAT)
    at = jnp.stack([pair_at, zh_at, tok_at, lax.axis_index("y"), lat_at]).astype(jnp.int32)

    quarter = swap(lax.dynamic_slice_in_dim(act, x_at * 16, 16, 0), "zh")
    near = gather(act, "y").reshape(256, D)
    far = gather(quarter, ("y", "x")).reshape(256, D)

    dec_wide = dec.astype(F32)
    nsq_part = jnp.sum(dec_wide * dec_wide, axis=1).reshape(8, own)

    def split(value):
        high = value.astype(BF)
        return [high, (value - high.astype(F32)).astype(BF)]

    thresh_level = thresholds.astype(F32) * 0.25

    parts, chunk = 4, D // 4
    encode = call(
        encode_kernel,
        "encode",
        2 * 256 * D * own,
        [((128, own), F32), ((128, own), F32)],
        0,
        [
            pltpu.VMEM((parts, 256, chunk), BF),
            pltpu.VMEM((parts, chunk, own), BF),
            pltpu.VMEM((256, own), F32),
            pltpu.SemaphoreType.DMA((2 * parts,)),
        ],
        2,
    )
    def halves(value):
        split_rows = value.reshape(16, 2, 8, value.shape[1])
        return [
            lax.dynamic_index_in_dim(split_rows, k, 1, False).reshape(128, value.shape[1])
            for k in (pair_at, 1 - pair_at)
        ]

    def features(acts, ahead):
        if ahead:
            keep, send = encode(at, acts, enc)
        else:
            keep, send = halves(jnp.dot(acts, enc, preferred_element_type=F32))
        pre = keep + swap(send, "pair") + enc_bias
        return (pre * jax.nn.sigmoid((pre - thresh_level) / smooth_width)).astype(BF)

    feats_near = features(near, True)
    nsq_two = [nsq_part, swap(nsq_part, "pair")]
    over = swap(
        jnp.concatenate([feats_near] + split(nsq_two[0]) + split(nsq_two[1]), axis=0), "zh"
    )
    over_near = over[:128]
    nsq_rows = []
    for k in range(2):
        rest = over[128 + 16 * k : 144 + 16 * k].astype(F32)
        nsq_rows += split(nsq_two[k] + rest[0:8] + rest[8:16])
    nsq_rows = lax.optimization_barrier(jnp.concatenate(nsq_rows, axis=0))
    dec_held, _ = lax.optimization_barrier((dec_t, feats_near))
    dec_oth = swap(dec_held, "pair")

    feats_far = features(far, False)
    over_far = swap(feats_far, "zh")
    g1 = gather(
        jnp.concatenate([feats_near, over_near, feats_far, nsq_rows], axis=0), "y"
    )
    over_far, g1 = lax.optimization_barrier((over_far, g1))
    g2 = gather(over_far, "y")

    payload, nsq_all = call(
        decode_kernel,
        "decode",
        2 * tokens * 8 * own * 512,
        [((tokens // 2, 1024), BF), ((8, own), F32)],
        4,
        [
            pltpu.VMEM((tokens // 2, 8 * own), BF),
            pltpu.VMEM((64, 8 * own), F32),
            pltpu.VMEM((64, 8 * own), BF),
        ],
        limit=40,
    )(at, g1, g2, dec_t, dec_oth)
    nsq_own = lax.dynamic_index_in_dim(nsq_all, tok_at, 0, keepdims=False)
    arrived = lax.all_to_all(payload.reshape(32, 8, 1024), LAT, 0, 0)

    cols = [
        halves(lax.dynamic_slice_in_dim(acts, tok_at * width, width, 1)) for acts in (near, far)
    ]
    own_acts = jnp.concatenate([cols[0][0], cols[1][0]], axis=0)
    bias_rows, rest = [], dec_bias
    for _ in range(3):
        bias_rows.append(rest.astype(BF))
        rest = rest - bias_rows[-1].astype(F32)
    sent = jnp.concatenate([cols[0][1], cols[1][1]] + bias_rows, axis=0)
    came = swap(sent, "pair")
    his_acts = came[:256]
    his_bias = jnp.sum(came[256:259].astype(F32), axis=0, keepdims=True)
    num_part, his_num, sum_sq = call(
        numer_kernel,
        "numer",
        2 * tokens * 8 * own * width,
        [((8, own), F32), ((8, own), F32), ((1, own), F32)],
        6,
        [],
        limit=40,
    )(at, g1, g2, dec_t, dec_oth, own_acts, his_acts)
    mean_sq = (sum_sq + swap(sum_sq, "pair"))[0] / tokens

    own_row = jnp.where((lat_at // 4) % 2 == zh_at, 0, 128)
    own_row = own_row + (lat_at // 8) * 32 + (lat_at % 4) * 8
    act_own, his_own = [
        lax.dynamic_slice_in_dim(acts, own_row, 8, 0) for acts in (own_acts, his_acts)
    ]
    recon_own, recon_his, last = call(
        close_kernel,
        "close",
        1 << 20,
        [((8, width), BF), ((8, width), BF), ((16, 4, 128), F32)],
        7,
        [],
        limit=16,
    )(at, arrived, dec_bias, his_bias, act_own, his_own, num_part, his_num)
    got = lax.all_to_all(last, ("pair",) + TOK, 0, 0, tiled=True)
    recon_came = swap(recon_his, "pair")
    recon = jnp.where(
        pair_at == 0,
        jnp.concatenate([recon_own, recon_came], axis=0),
        jnp.concatenate([recon_came, recon_own], axis=0),
    )
    token_loss = jnp.sum(got[:, 2, :rows], axis=0)
    num_own = jnp.sum(got[:, :2, :], axis=0).reshape(own) / tokens
    scaling = num_own / (nsq_own * mean_sq + tiny_term)
    return (recon[None], token_loss, scaling[None])


def solution(mesh):
    fine = Mesh(mesh.devices.reshape(2, 4, 8, 4, 2), ("pair", "x", "zl", "y", "zh"))
    return jax.shard_map(
        body,
        mesh=fine,
        in_specs=(
            P("pair", TOK, None),
            P("pair", None, LAT + TOK),
            P(LAT + TOK),
            P(LAT + TOK),
            P("pair", LAT, TOK),
            P("pair", TOK),
        ),
        out_specs=(P("pair", LAT, TOK), P(LAT), P("pair", LAT + TOK)),
        check_vma=False,
    )
```

```python
import jax
import jax.numpy as jnp
from jax import lax
from jax.experimental import pallas as pl
from jax.experimental.pallas import tpu as pltpu
from jax.sharding import Mesh, PartitionSpec as P

D = 3584
smooth_width = 0.1
penalty = 0.0001
tiny_term = 1e-06
LAT = ("x", "zl")
TOK = ("y", "zh")
BF = jnp.bfloat16
F32 = jnp.float32
VMEM = pl.BlockSpec(memory_space=pltpu.VMEM)
HBM = pl.BlockSpec(memory_space=pltpu.HBM)
SMEM = pl.BlockSpec(memory_space=pltpu.SMEM)
NT = (((1,), (1,)), ((), ()))


def swap(value, axis):
    return lax.ppermute(value, axis, [(0, 1), (1, 0)])


def gather(value, axes):
    size = lax.axis_size(axes)
    copies = jnp.broadcast_to(value[None], (size,) + value.shape)
    return lax.all_to_all(copies, axes, 0, 0, tiled=False)


def encode_kernel(at_ref, act_hbm, enc_hbm, keep_ref, send_ref, a_ref, enc_ref, v_ref, sems):
    pair_at = at_ref[0]
    count = a_ref.shape[0]
    chunk = a_ref.shape[2]
    loads = []
    for k in range(count):
        span = pl.ds(k * chunk, chunk)
        loads.append(
            (
                pltpu.make_async_copy(act_hbm.at[:, span], a_ref.at[k], sems.at[2 * k]),
                pltpu.make_async_copy(enc_hbm.at[span], enc_ref.at[k], sems.at[2 * k + 1]),
            )
        )
    for pair in loads:
        for copy in pair:
            copy.start()
    for k in range(count):
        for copy in loads[k]:
            copy.wait()
        part = jnp.dot(a_ref[k], enc_ref[k], preferred_element_type=F32)
        if k == 0:
            v_ref[...] = part
        else:
            v_ref[...] += part
    for j in range(16):
        rows = slice(j * 8, (j + 1) * 8)
        kept = pl.multiple_of(j * 16 + pair_at * 8, 8)
        sent = pl.multiple_of(j * 16 + (1 - pair_at) * 8, 8)
        keep_ref[rows, :] = v_ref[pl.ds(kept, 8), :]
        send_ref[rows, :] = v_ref[pl.ds(sent, 8), :]


def decode_kernel(
    at_ref, g1, g2, dec_ref, oth_ref, out_ref, nsq_ref, f_ref, wide_ref, norm_ref
):
    zh_at = at_ref[1]

    nsq = [jnp.zeros((8, 256), F32)] * 2
    for y in range(4):
        for at in (384, 416):
            rows = g1[y, at : at + 32, :].astype(F32)
            nsq[0] = nsq[0] + (rows[0:8] + rows[8:16])
            nsq[1] = nsq[1] + (rows[16:24] + rows[24:32])
    nsq_ref[...] = nsq[0]
    norm = (jnp.sqrt(nsq[0]) + jnp.sqrt(nsq[1])) * 0.125
    high = norm.astype(BF).astype(F32)
    wide_ref[...] = jnp.zeros_like(wide_ref)
    for k in range(8):
        wide_ref[0:1, k * 256 : (k + 1) * 256] = high[k : k + 1]
        wide_ref[1:2, k * 256 : (k + 1) * 256] = (norm - high)[k : k + 1]
    norm_ref[...] = wide_ref[...].astype(BF)

    for y in range(4):
        mine = pl.multiple_of((2 * y + zh_at) * 256, 256)
        theirs = pl.multiple_of((2 * y + 1 - zh_at) * 256, 256)
        f_ref[0:128, pl.ds(mine, 256)] = g1[y, 0:128, :]
        f_ref[128:256, pl.ds(theirs, 256)] = g1[y, 128:256, :]
        f_ref[128:256, pl.ds(mine, 256)] = g1[y, 256:384, :]
        f_ref[0:128, pl.ds(theirs, 256)] = g2[y]
    feats = f_ref[...]
    out = []
    for ref in (dec_ref, norm_ref, oth_ref):
        value = lax.dot_general(feats, ref[...], NT, preferred_element_type=F32)
        out.append(value.astype(BF))
    for half in range(2):
        zh = zh_at if half == 0 else 1 - zh_at
        for y in range(4):
            src = slice(half * 128 + y * 32, half * 128 + (y + 1) * 32)
            dst = pl.ds(pl.multiple_of((2 * y + zh) * 32, 32), 32)
            out_ref[dst, 0:448] = out[0][src]
            out_ref[dst, 448:512] = out[1][src]
            out_ref[dst, 512:960] = out[2][src]
            out_ref[dst, 960:1024] = jnp.zeros((32, 64), BF)


def numer_kernel(
    at_ref, g1, g2, dec_ref, oth_ref, own_ref, his_ref, num_ref, his_num_ref, msq_ref
):
    zh_at, y_at = at_ref[1], at_ref[3]
    for acts, dec, num in ((own_ref, dec_ref, num_ref), (his_ref, oth_ref, his_num_ref)):
        for y in range(4):
            for zh in range(2):
                at = 2 * y + (zh_at if zh == 0 else 1 - zh_at)
                cols = dec[:, pl.ds(pl.multiple_of(at * 256, 256), 256)]
                inner = jnp.dot(acts[...], cols, preferred_element_type=F32)
                near = g1[y, 0:128, :] if zh == 0 else g2[y]
                far = g1[y, 256:384, :] if zh == 0 else g1[y, 128:256, :]
                both = inner[0:128] * near.astype(F32) + inner[128:256] * far.astype(F32)
                num[pl.ds(at, 1), :] = jnp.sum(both, axis=0, keepdims=True)

    squares = jnp.zeros((128, 256), F32)
    for rows in (slice(0, 128), slice(256, 384)):
        feats = g1[y_at, rows, :].astype(F32)
        squares = squares + feats * feats
    msq_ref[...] = jnp.sum(squares, axis=0, keepdims=True)


def close_kernel(
    at_ref,
    arrived_ref,
    bias_ref,
    his_bias_ref,
    act_ref,
    his_act_ref,
    num_ref,
    his_num_ref,
    recon_ref,
    his_recon_ref,
    last_ref,
):
    pair_at = at_ref[0]
    total = arrived_ref[0].astype(F32)
    for k in range(1, 32):
        total = total + arrived_ref[k].astype(F32)
    terms = penalty * (total[:, 448:449] + total[:, 449:450])
    for at, bias, act, out in (
        (0, bias_ref, act_ref, recon_ref),
        (512, his_bias_ref, his_act_ref, his_recon_ref),
    ):
        recon = total[:, at : at + 448] + bias[...]
        out[...] = recon.astype(BF)
        residue = act[...].astype(F32) - recon
        terms = terms + jnp.sum(residue * residue, axis=1, keepdims=True) / (2.0 * D)
    row = lax.broadcasted_iota(jnp.int32, (8, 128), 0)
    lane = lax.broadcasted_iota(jnp.int32, (8, 128), 1)
    line = jnp.sum(jnp.where(row + pair_at * 8 == lane, terms, 0.0), axis=0, keepdims=True)
    for pair in range(2):
        num = jnp.where(pair_at == pair, num_ref[...], his_num_ref[...])
        for k in range(8):
            at = pair * 8 + k
            last_ref[at, 0:1, :] = num[k : k + 1, 0:128]
            last_ref[at, 1:2, :] = num[k : k + 1, 128:256]
            last_ref[at, 2:3, :] = line
            last_ref[at, 3:4, :] = line


def call(kernel, name, flops, outs, count, scratch, outside=0, limit=60):
    return pl.pallas_call(
        kernel,
        out_shape=tuple(jax.ShapeDtypeStruct(shape, kind) for shape, kind in outs),
        in_specs=[SMEM] + [VMEM] * count + [HBM] * outside,
        out_specs=(VMEM,) * len(outs),
        scratch_shapes=scratch,
        compiler_params=pltpu.CompilerParams(vmem_limit_bytes=limit << 20),
        cost_estimate=pl.CostEstimate(
            flops=flops, bytes_accessed=6 << 20, transcendentals=0
        ),
        name=name,
    )


def body(activations, enc_weight, enc_bias, thresholds, dec_weight, dec_bias):
    pair_at = lax.axis_index("pair")
    x_at = lax.axis_index("x")
    zh_at = lax.axis_index("zh")
    tok_at = lax.axis_index(TOK)
    lat_at = lax.axis_index(LAT)
    act = activations[0]
    enc = enc_weight[0]
    dec = dec_weight[0]
    dec_t = dec.T
    own, width = enc.shape[1], dec.shape[1]
    tokens = 8 * act.shape[0]
    rows = tokens // lax.axis_size(LAT)
    at = jnp.stack([pair_at, zh_at, tok_at, lax.axis_index("y"), lat_at]).astype(jnp.int32)

    quarter = swap(lax.dynamic_slice_in_dim(act, x_at * 16, 16, 0), "zh")
    dec_wide = dec.astype(F32)
    nsq_part = jnp.sum(dec_wide * dec_wide, axis=1).reshape(8, own)
    nsq_two = [nsq_part, swap(nsq_part, "pair")]
    quarter, nsq_two[0], nsq_two[1], at = lax.optimization_barrier((quarter, *nsq_two, at))

    near = gather(act, "y").reshape(256, D)
    far = gather(quarter, ("y", "x")).reshape(256, D)

    def split(value):
        high = value.astype(BF)
        return [high, (value - high.astype(F32)).astype(BF)]

    thresh_level = thresholds.astype(F32) * 0.25

    parts, chunk = 4, D // 4
    encode = call(
        encode_kernel,
        "encode",
        2 * 256 * D * own,
        [((128, own), F32), ((128, own), F32)],
        0,
        [
            pltpu.VMEM((parts, 256, chunk), BF),
            pltpu.VMEM((parts, chunk, own), BF),
            pltpu.VMEM((256, own), F32),
            pltpu.SemaphoreType.DMA((2 * parts,)),
        ],
        2,
    )
    def halves(value):
        split_rows = value.reshape(16, 2, 8, value.shape[1])
        return [
            lax.dynamic_index_in_dim(split_rows, k, 1, False).reshape(128, value.shape[1])
            for k in (pair_at, 1 - pair_at)
        ]

    def features(keep, came):
        pre = keep + came + enc_bias
        return (pre * jax.nn.sigmoid((pre - thresh_level) / smooth_width)).astype(BF)

    keep, send = encode(at, near, enc)
    feats_near = features(keep, swap(send, "pair"))
    nsq_rows = lax.optimization_barrier(
        jnp.concatenate(split(nsq_two[0]) + split(nsq_two[1]), axis=0)
    )
    over = swap(jnp.concatenate([feats_near, nsq_rows], axis=0), "zh")
    dec_held, _ = lax.optimization_barrier((dec_t, feats_near))
    dec_oth = swap(dec_held, "pair")

    part_far = jnp.dot(far, enc, preferred_element_type=F32)
    keep, send = halves(part_far)
    over, keep = lax.optimization_barrier((over, keep))
    feats_far = features(keep, swap(send, "pair"))
    over_far = swap(feats_far, "zh")
    g1 = gather(
        jnp.concatenate([feats_near, over[:128], feats_far, nsq_rows, over[128:]], axis=0), "y"
    )
    over_far, g1 = lax.optimization_barrier((over_far, g1))
    g2 = gather(over_far, "y")

    payload, nsq_all = call(
        decode_kernel,
        "decode",
        2 * tokens * 8 * own * 512,
        [((tokens // 2, 1024), BF), ((8, own), F32)],
        4,
        [
            pltpu.VMEM((tokens // 2, 8 * own), BF),
            pltpu.VMEM((64, 8 * own), F32),
            pltpu.VMEM((64, 8 * own), BF),
        ],
        limit=40,
    )(at, g1, g2, dec_t, dec_oth)
    nsq_own = lax.dynamic_index_in_dim(nsq_all, tok_at, 0, keepdims=False)
    arrived = lax.all_to_all(payload.reshape(32, 8, 1024), LAT, 0, 0)

    cols = [
        halves(lax.dynamic_slice_in_dim(acts, tok_at * width, width, 1)) for acts in (near, far)
    ]
    own_acts = jnp.concatenate([cols[0][0], cols[1][0]], axis=0)
    bias_rows, rest = [], dec_bias
    for _ in range(3):
        bias_rows.append(rest.astype(BF))
        rest = rest - bias_rows[-1].astype(F32)
    bias_rows = jnp.pad(jnp.concatenate(bias_rows, axis=0), ((0, 13), (0, 0)))
    sent = jnp.concatenate([cols[0][1], cols[1][1], bias_rows], axis=0)
    came = swap(sent, "pair")
    his_acts = came[:256]
    his_bias = jnp.sum(came[256:259].astype(F32), axis=0, keepdims=True)
    num_part, his_num, sum_sq = call(
        numer_kernel,
        "numer",
        2 * tokens * 8 * own * width,
        [((8, own), F32), ((8, own), F32), ((1, own), F32)],
        6,
        [],
        limit=40,
    )(at, g1, g2, dec_t, dec_oth, own_acts, his_acts)
    mean_sq = (sum_sq + swap(sum_sq, "pair"))[0] / tokens

    own_row = jnp.where((lat_at // 4) % 2 == zh_at, 0, 128)
    own_row = own_row + (lat_at // 8) * 32 + (lat_at % 4) * 8
    act_own, his_own = [
        lax.dynamic_slice_in_dim(acts, own_row, 8, 0) for acts in (own_acts, his_acts)
    ]
    recon_own, recon_his, last = call(
        close_kernel,
        "close",
        1 << 20,
        [((8, width), BF), ((8, width), BF), ((16, 4, 128), F32)],
        7,
        [],
        limit=16,
    )(at, arrived, dec_bias, his_bias, act_own, his_own, num_part, his_num)
    got = lax.all_to_all(last, ("pair",) + TOK, 0, 0, tiled=True)
    recon_came = swap(recon_his, "pair")
    recon = jnp.where(
        pair_at == 0,
        jnp.concatenate([recon_own, recon_came], axis=0),
        jnp.concatenate([recon_came, recon_own], axis=0),
    )
    token_loss = jnp.sum(got[:, 2, :rows], axis=0)
    num_own = jnp.sum(got[:, :2, :], axis=0).reshape(own) / tokens
    scaling = num_own / (nsq_own * mean_sq + tiny_term)
    return (recon[None], token_loss, scaling[None])


def solution(mesh):
    fine = Mesh(mesh.devices.reshape(2, 4, 8, 4, 2), ("pair", "x", "zl", "y", "zh"))
    return jax.shard_map(
        body,
        mesh=fine,
        in_specs=(
            P("pair", TOK, None),
            P("pair", None, LAT + TOK),
            P(LAT + TOK),
            P(LAT + TOK),
            P("pair", LAT, TOK),
            P("pair", TOK),
        ),
        out_specs=(P("pair", LAT, TOK), P(LAT), P("pair", LAT + TOK)),
        check_vma=False,
    )
```

```python
import jax
import jax.numpy as jnp
from jax import lax
from jax.experimental import pallas as pl
from jax.experimental.pallas import tpu as pltpu
from jax.sharding import Mesh, PartitionSpec as P

D = 3584
smooth_width = 0.1
penalty = 0.0001
tiny_term = 1e-06
LAT = ("x", "zl")
TOK = ("y", "zh")
BF = jnp.bfloat16
F32 = jnp.float32
VMEM = pl.BlockSpec(memory_space=pltpu.VMEM)
HBM = pl.BlockSpec(memory_space=pltpu.HBM)
SMEM = pl.BlockSpec(memory_space=pltpu.SMEM)
NT = (((1,), (1,)), ((), ()))


def swap(value, axis):
    return lax.ppermute(value, axis, [(0, 1), (1, 0)])


def gather(value, axes):
    size = lax.axis_size(axes)
    copies = jnp.broadcast_to(value[None], (size,) + value.shape)
    return lax.all_to_all(copies, axes, 0, 0, tiled=False)


def encode_kernel(at_ref, act_hbm, enc_hbm, keep_ref, send_ref, a_ref, enc_ref, v_ref, sems):
    pair_at = at_ref[0]
    count = a_ref.shape[0]
    chunk = a_ref.shape[2]
    loads = []
    for k in range(count):
        span = pl.ds(k * chunk, chunk)
        loads.append(
            (
                pltpu.make_async_copy(act_hbm.at[:, span], a_ref.at[k], sems.at[2 * k]),
                pltpu.make_async_copy(enc_hbm.at[span], enc_ref.at[k], sems.at[2 * k + 1]),
            )
        )
    for pair in loads:
        for copy in pair:
            copy.start()
    for k in range(count):
        for copy in loads[k]:
            copy.wait()
        part = jnp.dot(a_ref[k], enc_ref[k], preferred_element_type=F32)
        if k == 0:
            v_ref[...] = part
        else:
            v_ref[...] += part
    for j in range(16):
        rows = slice(j * 8, (j + 1) * 8)
        kept = pl.multiple_of(j * 16 + pair_at * 8, 8)
        sent = pl.multiple_of(j * 16 + (1 - pair_at) * 8, 8)
        keep_ref[rows, :] = v_ref[pl.ds(kept, 8), :]
        send_ref[rows, :] = v_ref[pl.ds(sent, 8), :]


def norms_of(g1):
    nsq = [jnp.zeros((8, 256), F32)] * 2
    for y in range(4):
        for at in (384, 416):
            rows = g1[y, at : at + 32, :].astype(F32)
            nsq[0] = nsq[0] + (rows[0:8] + rows[8:16])
            nsq[1] = nsq[1] + (rows[16:24] + rows[24:32])
    return nsq


def decode_kernel(
    at_ref, g1, g2, dec_ref, oth_ref, out_ref, f_ref, wide_ref, norm_ref
):
    zh_at = at_ref[1]

    nsq = norms_of(g1)
    norm = (jnp.sqrt(nsq[0]) + jnp.sqrt(nsq[1])) * 0.125
    high = norm.astype(BF).astype(F32)
    wide_ref[...] = jnp.zeros_like(wide_ref)
    for k in range(8):
        wide_ref[0:1, k * 256 : (k + 1) * 256] = high[k : k + 1]
        wide_ref[1:2, k * 256 : (k + 1) * 256] = (norm - high)[k : k + 1]
    norm_ref[...] = wide_ref[...].astype(BF)

    for y in range(4):
        mine = pl.multiple_of((2 * y + zh_at) * 256, 256)
        theirs = pl.multiple_of((2 * y + 1 - zh_at) * 256, 256)
        f_ref[0:128, pl.ds(mine, 256)] = g1[y, 0:128, :]
        f_ref[128:256, pl.ds(theirs, 256)] = g1[y, 128:256, :]
        f_ref[128:256, pl.ds(mine, 256)] = g1[y, 256:384, :]
        f_ref[0:128, pl.ds(theirs, 256)] = g2[y]
    feats = f_ref[...]
    out = []
    for ref in (dec_ref, norm_ref, oth_ref):
        value = lax.dot_general(feats, ref[...], NT, preferred_element_type=F32)
        out.append(value.astype(BF))
    for half in range(2):
        zh = zh_at if half == 0 else 1 - zh_at
        for y in range(4):
            src = slice(half * 128 + y * 32, half * 128 + (y + 1) * 32)
            dst = pl.ds(pl.multiple_of((2 * y + zh) * 32, 32), 32)
            out_ref[dst, 0:448] = out[0][src]
            out_ref[dst, 448:512] = out[1][src]
            out_ref[dst, 512:960] = out[2][src]
            out_ref[dst, 960:1024] = jnp.zeros((32, 64), BF)


def numer_kernel(
    at_ref,
    g1,
    g2,
    dec_ref,
    oth_ref,
    own_ref,
    his_ref,
    bias_ref,
    pack_ref,
    stat_ref,
    num_ref,
    nsq_ref,
):
    zh_at, tok_at, y_at, lat_at = [at_ref[k] for k in range(1, 5)]
    for k, (acts, dec) in enumerate(((own_ref, dec_ref), (his_ref, oth_ref))):
        rows = acts[0:256, :]
        for y in range(4):
            for zh in range(2):
                at = 2 * y + (zh_at if zh == 0 else 1 - zh_at)
                cols = dec[:, pl.ds(pl.multiple_of(at * 256, 256), 256)]
                inner = jnp.dot(rows, cols, preferred_element_type=F32)
                near = g1[y, 0:128, :] if zh == 0 else g2[y]
                far = g1[y, 256:384, :] if zh == 0 else g1[y, 128:256, :]
                both = inner[0:128] * near.astype(F32) + inner[128:256] * far.astype(F32)
                num_ref[k, pl.ds(at, 1), :] = jnp.sum(both, axis=0, keepdims=True)
    pack_ref[0:8, 0:256] = num_ref[0]
    pack_ref[0:8, 256:512] = num_ref[1]

    row = (lat_at // 8) * 32 + (lat_at % 4) * 8
    row = row + jnp.where((lat_at // 4) % 2 == zh_at, 0, 128)
    for k, acts in enumerate((own_ref, his_ref)):
        rows = acts[pl.ds(pl.multiple_of((row // 16) * 16, 16), 16), :].astype(F32)
        kept = jnp.where((row // 8) % 2 == 0, rows[0:8], rows[8:16])
        pack_ref[8 + 8 * k : 16 + 8 * k, 0:448] = kept
    pack_ref[24:25, 0:448] = bias_ref[...]
    rows = his_ref[256:272, :].astype(F32)
    pack_ref[25:26, 0:448] = (rows[0:1] + rows[1:2]) + rows[2:3]

    squares = jnp.zeros((128, 256), F32)
    for rows in (slice(0, 128), slice(256, 384)):
        feats = g1[y_at, rows, :].astype(F32)
        squares = squares + feats * feats
    nsq_ref[...] = norms_of(g1)[0]
    stat_ref[0:1, :] = jnp.sum(squares, axis=0, keepdims=True)
    stat_ref[1:2, :] = nsq_ref[pl.ds(tok_at, 1), :]


def close_kernel(at_ref, arrived_ref, pack_ref, recon_ref, his_recon_ref, last_ref):
    pair_at = at_ref[0]
    total = arrived_ref[0].astype(F32)
    for k in range(1, 32):
        total = total + arrived_ref[k].astype(F32)
    terms = penalty * (total[:, 448:449] + total[:, 449:450])
    for k, out in enumerate((recon_ref, his_recon_ref)):
        recon = total[:, 512 * k : 512 * k + 448] + pack_ref[24 + k : 25 + k, 0:448]
        out[...] = recon.astype(BF)
        residue = pack_ref[8 + 8 * k : 16 + 8 * k, 0:448] - recon
        terms = terms + jnp.sum(residue * residue, axis=1, keepdims=True) / (2.0 * D)
    row = lax.broadcasted_iota(jnp.int32, (8, 128), 0)
    lane = lax.broadcasted_iota(jnp.int32, (8, 128), 1)
    line = jnp.sum(jnp.where(row + pair_at * 8 == lane, terms, 0.0), axis=0, keepdims=True)
    for pair in range(2):
        num = jnp.where(pair_at == pair, pack_ref[0:8, 0:256], pack_ref[0:8, 256:512])
        for k in range(8):
            at = pair * 8 + k
            last_ref[at, 0:1, :] = num[k : k + 1, 0:128]
            last_ref[at, 1:2, :] = num[k : k + 1, 128:256]
            last_ref[at, 2:3, :] = line
            last_ref[at, 3:4, :] = line


def call(kernel, name, flops, outs, count, scratch, outside=0, limit=60):
    return pl.pallas_call(
        kernel,
        out_shape=tuple(jax.ShapeDtypeStruct(shape, kind) for shape, kind in outs),
        in_specs=[SMEM] + [VMEM] * count + [HBM] * outside,
        out_specs=(VMEM,) * len(outs),
        scratch_shapes=scratch,
        compiler_params=pltpu.CompilerParams(vmem_limit_bytes=limit << 20),
        cost_estimate=pl.CostEstimate(
            flops=flops, bytes_accessed=6 << 20, transcendentals=0
        ),
        name=name,
    )


def body(activations, enc_weight, enc_bias, thresholds, dec_weight, dec_bias):
    pair_at = lax.axis_index("pair")
    x_at = lax.axis_index("x")
    zh_at = lax.axis_index("zh")
    tok_at = lax.axis_index(TOK)
    lat_at = lax.axis_index(LAT)
    act = activations[0]
    enc = enc_weight[0]
    dec = dec_weight[0]
    dec_t = dec.T
    own, width = enc.shape[1], dec.shape[1]
    tokens = 8 * act.shape[0]
    rows = tokens // lax.axis_size(LAT)
    at = jnp.stack([pair_at, zh_at, tok_at, lax.axis_index("y"), lat_at]).astype(jnp.int32)

    quarter = swap(lax.dynamic_slice_in_dim(act, x_at * 16, 16, 0), "zh")
    dec_wide = dec.astype(F32)
    nsq_part = jnp.sum(dec_wide * dec_wide, axis=1).reshape(8, own)
    nsq_two = [nsq_part, swap(nsq_part, "pair")]
    quarter, nsq_two[0], nsq_two[1], at = lax.optimization_barrier((quarter, *nsq_two, at))

    near = gather(act, "y").reshape(256, D)
    far = gather(quarter, ("y", "x")).reshape(256, D)

    def split(value):
        high = value.astype(BF)
        return [high, (value - high.astype(F32)).astype(BF)]

    thresh_level = thresholds.astype(F32) * 0.25

    parts, chunk = 4, D // 4
    encode = call(
        encode_kernel,
        "encode",
        2 * 256 * D * own,
        [((128, own), F32), ((128, own), F32)],
        0,
        [
            pltpu.VMEM((parts, 256, chunk), BF),
            pltpu.VMEM((parts, chunk, own), BF),
            pltpu.VMEM((256, own), F32),
            pltpu.SemaphoreType.DMA((2 * parts,)),
        ],
        2,
    )
    def halves(value):
        split_rows = value.reshape(16, 2, 8, value.shape[1])
        return [
            lax.dynamic_index_in_dim(split_rows, k, 1, False).reshape(128, value.shape[1])
            for k in (pair_at, 1 - pair_at)
        ]

    def features(keep, came):
        pre = keep + came + enc_bias
        return (pre * jax.nn.sigmoid((pre - thresh_level) / smooth_width)).astype(BF)

    keep, send = encode(at, near, enc)
    feats_near = features(keep, swap(send, "pair"))
    nsq_rows = lax.optimization_barrier(
        jnp.concatenate(split(nsq_two[0]) + split(nsq_two[1]), axis=0)
    )
    over = swap(jnp.concatenate([feats_near, nsq_rows], axis=0), "zh")
    dec_held, _ = lax.optimization_barrier((dec_t, feats_near))
    dec_oth = swap(dec_held, "pair")

    part_far = jnp.dot(far, enc, preferred_element_type=F32)
    keep, send = halves(part_far)
    over, keep = lax.optimization_barrier((over, keep))
    feats_far = features(keep, swap(send, "pair"))
    over_far = swap(feats_far, "zh")
    g1 = gather(
        jnp.concatenate([feats_near, over[:128], feats_far, nsq_rows, over[128:]], axis=0), "y"
    )
    over_far, g1 = lax.optimization_barrier((over_far, g1))
    g2 = gather(over_far, "y")

    (payload,) = call(
        decode_kernel,
        "decode",
        2 * tokens * 8 * own * 512,
        [((tokens // 2, 1024), BF)],
        4,
        [
            pltpu.VMEM((tokens // 2, 8 * own), BF),
            pltpu.VMEM((64, 8 * own), F32),
            pltpu.VMEM((64, 8 * own), BF),
        ],
        limit=40,
    )(at, g1, g2, dec_t, dec_oth)
    arrived = lax.all_to_all(payload.reshape(32, 8, 1024), LAT, 0, 0)

    cols = [
        halves(lax.dynamic_slice_in_dim(acts, tok_at * width, width, 1)) for acts in (near, far)
    ]
    own_acts = jnp.concatenate([cols[0][0], cols[1][0]], axis=0)
    bias_rows, rest = [], dec_bias
    for _ in range(3):
        bias_rows.append(rest.astype(BF))
        rest = rest - bias_rows[-1].astype(F32)
    bias_rows = jnp.pad(jnp.concatenate(bias_rows, axis=0), ((0, 13), (0, 0)))
    sent = jnp.concatenate([cols[0][1], cols[1][1], bias_rows], axis=0)
    came = swap(sent, "pair")
    pack, stats = call(
        numer_kernel,
        "numer",
        2 * tokens * 8 * own * width,
        [((32, 512), F32), ((2, own), F32)],
        7,
        [pltpu.VMEM((2, 8, own), F32), pltpu.VMEM((8, own), F32)],
        limit=40,
    )(at, g1, g2, dec_t, dec_oth, own_acts, came, dec_bias)
    nsq_own = stats[1]
    mean_sq = (stats[:1] + swap(stats[:1], "pair"))[0] / tokens

    recon_own, recon_his, last = call(
        close_kernel,
        "close",
        1 << 20,
        [((8, width), BF), ((8, width), BF), ((16, 4, 128), F32)],
        2,
        [],
        limit=16,
    )(at, arrived, pack)
    got = lax.all_to_all(last, ("pair",) + TOK, 0, 0, tiled=True)
    recon_came = swap(recon_his, "pair")
    recon = jnp.where(
        pair_at == 0,
        jnp.concatenate([recon_own, recon_came], axis=0),
        jnp.concatenate([recon_came, recon_own], axis=0),
    )
    token_loss = jnp.sum(got[:, 2, :rows], axis=0)
    num_own = jnp.sum(got[:, :2, :], axis=0).reshape(own) / tokens
    scaling = num_own / (nsq_own * mean_sq + tiny_term)
    return (recon[None], token_loss, scaling[None])


def solution(mesh):
    fine = Mesh(mesh.devices.reshape(2, 4, 8, 4, 2), ("pair", "x", "zl", "y", "zh"))
    return jax.shard_map(
        body,
        mesh=fine,
        in_specs=(
            P("pair", TOK, None),
            P("pair", None, LAT + TOK),
            P(LAT + TOK),
            P(LAT + TOK),
            P("pair", LAT, TOK),
            P("pair", TOK),
        ),
        out_specs=(P("pair", LAT, TOK), P(LAT), P("pair", LAT + TOK)),
        check_vma=False,
    )
```

```python
import jax
import jax.numpy as jnp
from jax import lax
from jax.experimental import pallas as pl
from jax.experimental.pallas import tpu as pltpu
from jax.sharding import Mesh, PartitionSpec as P

D = 3584
smooth_width = 0.1
penalty = 0.0001
tiny_term = 1e-06
LAT = ("x", "zl")
TOK = ("y", "zh")
BF = jnp.bfloat16
F32 = jnp.float32
VMEM = pl.BlockSpec(memory_space=pltpu.VMEM)
HBM = pl.BlockSpec(memory_space=pltpu.HBM)
SMEM = pl.BlockSpec(memory_space=pltpu.SMEM)
NT = (((1,), (1,)), ((), ()))


def swap(value, axis):
    return lax.ppermute(value, axis, [(0, 1), (1, 0)])


def gather(value, axes):
    size = lax.axis_size(axes)
    copies = jnp.broadcast_to(value[None], (size,) + value.shape)
    return lax.all_to_all(copies, axes, 0, 0, tiled=False)


def encode_kernel(at_ref, act_hbm, enc_hbm, keep_ref, send_ref, a_ref, enc_ref, v_ref, sems):
    pair_at = at_ref[0]
    count = a_ref.shape[0]
    chunk = a_ref.shape[2]
    loads = []
    for k in range(count):
        span = pl.ds(k * chunk, chunk)
        loads.append(
            (
                pltpu.make_async_copy(act_hbm.at[:, span], a_ref.at[k], sems.at[2 * k]),
                pltpu.make_async_copy(enc_hbm.at[span], enc_ref.at[k], sems.at[2 * k + 1]),
            )
        )
    for pair in loads:
        for copy in pair:
            copy.start()
    for k in range(count):
        for copy in loads[k]:
            copy.wait()
        part = jnp.dot(a_ref[k], enc_ref[k], preferred_element_type=F32)
        if k == 0:
            v_ref[...] = part
        else:
            v_ref[...] += part
    for j in range(16):
        rows = slice(j * 8, (j + 1) * 8)
        kept = pl.multiple_of(j * 16 + pair_at * 8, 8)
        sent = pl.multiple_of(j * 16 + (1 - pair_at) * 8, 8)
        keep_ref[rows, :] = v_ref[pl.ds(kept, 8), :]
        send_ref[rows, :] = v_ref[pl.ds(sent, 8), :]


def norms_of(g1):
    nsq = [jnp.zeros((8, 256), F32)] * 2
    for y in range(4):
        for at in (384, 416):
            rows = g1[y, at : at + 32, :].astype(F32)
            nsq[0] = nsq[0] + (rows[0:8] + rows[8:16])
            nsq[1] = nsq[1] + (rows[16:24] + rows[24:32])
    return nsq


def decode_kernel(at_ref, g1, dec_ref, oth_ref, part_ref, norm_ref, f_ref, wide_ref):
    zh_at = at_ref[1]

    nsq = norms_of(g1)
    norm = (jnp.sqrt(nsq[0]) + jnp.sqrt(nsq[1])) * 0.125
    high = norm.astype(BF).astype(F32)
    wide_ref[...] = jnp.zeros_like(wide_ref)
    for k in range(8):
        wide_ref[0:1, k * 256 : (k + 1) * 256] = high[k : k + 1]
        wide_ref[1:2, k * 256 : (k + 1) * 256] = (norm - high)[k : k + 1]
    norm_ref[...] = wide_ref[...].astype(BF)

    for y in range(4):
        mine = pl.multiple_of((2 * y + zh_at) * 256, 256)
        theirs = pl.multiple_of((2 * y + 1 - zh_at) * 256, 256)
        f_ref[0:128, pl.ds(mine, 256)] = g1[y, 0:128, :]
        f_ref[128:256, pl.ds(theirs, 256)] = g1[y, 128:256, :]
        f_ref[128:256, pl.ds(mine, 256)] = g1[y, 256:384, :]
        f_ref[0:128, pl.ds(theirs, 256)] = jnp.zeros((128, 256), BF)
    feats = f_ref[...]
    for ref, at, width in ((dec_ref, 0, 448), (norm_ref, 448, 64), (oth_ref, 512, 448)):
        value = lax.dot_general(feats, ref[...], NT, preferred_element_type=F32)
        part_ref[:, at : at + width] = value
    part_ref[:, 960:1024] = jnp.zeros((256, 64), F32)


def finish_kernel(at_ref, g2, dec_ref, oth_ref, norm_ref, part_ref, out_ref):
    zh_at = at_ref[1]
    for ref, at, width in ((dec_ref, 0, 448), (norm_ref, 448, 64), (oth_ref, 512, 448)):
        value = part_ref[0:128, at : at + width]
        for y in range(4):
            theirs = pl.multiple_of((2 * y + 1 - zh_at) * 256, 256)
            cols = ref[:, pl.ds(theirs, 256)]
            value = value + lax.dot_general(g2[y], cols, NT, preferred_element_type=F32)
        value = value.astype(BF)
        for y in range(4):
            dst = pl.ds(pl.multiple_of((2 * y + zh_at) * 32, 32), 32)
            out_ref[dst, at : at + width] = value[y * 32 : (y + 1) * 32]
    for y in range(4):
        dst = pl.ds(pl.multiple_of((2 * y + 1 - zh_at) * 32, 32), 32)
        src = slice(128 + y * 32, 128 + (y + 1) * 32)
        out_ref[dst, :] = part_ref[src, :].astype(BF)
        near = pl.ds(pl.multiple_of((2 * y + zh_at) * 32, 32), 32)
        out_ref[near, 960:1024] = jnp.zeros((32, 64), BF)


def numer_kernel(
    at_ref,
    g1,
    g2,
    dec_ref,
    oth_ref,
    own_ref,
    his_ref,
    bias_ref,
    pack_ref,
    stat_ref,
    num_ref,
    nsq_ref,
):
    zh_at, tok_at, y_at, lat_at = [at_ref[k] for k in range(1, 5)]
    for k, (acts, dec) in enumerate(((own_ref, dec_ref), (his_ref, oth_ref))):
        rows = acts[0:256, :]
        for y in range(4):
            for zh in range(2):
                at = 2 * y + (zh_at if zh == 0 else 1 - zh_at)
                cols = dec[:, pl.ds(pl.multiple_of(at * 256, 256), 256)]
                inner = jnp.dot(rows, cols, preferred_element_type=F32)
                near = g1[y, 0:128, :] if zh == 0 else g2[y]
                far = g1[y, 256:384, :] if zh == 0 else g1[y, 128:256, :]
                both = inner[0:128] * near.astype(F32) + inner[128:256] * far.astype(F32)
                num_ref[k, pl.ds(at, 1), :] = jnp.sum(both, axis=0, keepdims=True)
    pack_ref[0:8, 0:256] = num_ref[0]
    pack_ref[0:8, 256:512] = num_ref[1]

    row = (lat_at // 8) * 32 + (lat_at % 4) * 8
    row = row + jnp.where((lat_at // 4) % 2 == zh_at, 0, 128)
    for k, acts in enumerate((own_ref, his_ref)):
        rows = acts[pl.ds(pl.multiple_of((row // 16) * 16, 16), 16), :].astype(F32)
        kept = jnp.where((row // 8) % 2 == 0, rows[0:8], rows[8:16])
        pack_ref[8 + 8 * k : 16 + 8 * k, 0:448] = kept
    pack_ref[24:25, 0:448] = bias_ref[...]
    rows = his_ref[256:272, :].astype(F32)
    pack_ref[25:26, 0:448] = (rows[0:1] + rows[1:2]) + rows[2:3]

    squares = jnp.zeros((128, 256), F32)
    for rows in (slice(0, 128), slice(256, 384)):
        feats = g1[y_at, rows, :].astype(F32)
        squares = squares + feats * feats
    nsq_ref[...] = norms_of(g1)[0]
    stat_ref[0:1, :] = jnp.sum(squares, axis=0, keepdims=True)
    stat_ref[1:2, :] = nsq_ref[pl.ds(tok_at, 1), :]


def close_kernel(at_ref, arrived_ref, pack_ref, recon_ref, his_recon_ref, last_ref):
    pair_at = at_ref[0]
    total = arrived_ref[0].astype(F32)
    for k in range(1, 32):
        total = total + arrived_ref[k].astype(F32)
    terms = penalty * (total[:, 448:449] + total[:, 449:450])
    for k, out in enumerate((recon_ref, his_recon_ref)):
        recon = total[:, 512 * k : 512 * k + 448] + pack_ref[24 + k : 25 + k, 0:448]
        out[...] = recon.astype(BF)
        residue = pack_ref[8 + 8 * k : 16 + 8 * k, 0:448] - recon
        terms = terms + jnp.sum(residue * residue, axis=1, keepdims=True) / (2.0 * D)
    row = lax.broadcasted_iota(jnp.int32, (8, 128), 0)
    lane = lax.broadcasted_iota(jnp.int32, (8, 128), 1)
    line = jnp.sum(jnp.where(row + pair_at * 8 == lane, terms, 0.0), axis=0, keepdims=True)
    for pair in range(2):
        num = jnp.where(pair_at == pair, pack_ref[0:8, 0:256], pack_ref[0:8, 256:512])
        for k in range(8):
            at = pair * 8 + k
            last_ref[at, 0:1, :] = num[k : k + 1, 0:128]
            last_ref[at, 1:2, :] = num[k : k + 1, 128:256]
            last_ref[at, 2:3, :] = line
            last_ref[at, 3:4, :] = line


def call(kernel, name, flops, outs, count, scratch, outside=0, limit=60):
    return pl.pallas_call(
        kernel,
        out_shape=tuple(jax.ShapeDtypeStruct(shape, kind) for shape, kind in outs),
        in_specs=[SMEM] + [VMEM] * count + [HBM] * outside,
        out_specs=(VMEM,) * len(outs),
        scratch_shapes=scratch,
        compiler_params=pltpu.CompilerParams(vmem_limit_bytes=limit << 20),
        cost_estimate=pl.CostEstimate(
            flops=flops, bytes_accessed=6 << 20, transcendentals=0
        ),
        name=name,
    )


def body(activations, enc_weight, enc_bias, thresholds, dec_weight, dec_bias):
    pair_at = lax.axis_index("pair")
    x_at = lax.axis_index("x")
    zh_at = lax.axis_index("zh")
    tok_at = lax.axis_index(TOK)
    lat_at = lax.axis_index(LAT)
    act = activations[0]
    enc = enc_weight[0]
    dec = dec_weight[0]
    dec_t = dec.T
    own, width = enc.shape[1], dec.shape[1]
    tokens = 8 * act.shape[0]
    rows = tokens // lax.axis_size(LAT)
    at = jnp.stack([pair_at, zh_at, tok_at, lax.axis_index("y"), lat_at]).astype(jnp.int32)

    quarter = swap(lax.dynamic_slice_in_dim(act, x_at * 16, 16, 0), "zh")
    dec_wide = dec.astype(F32)
    nsq_part = jnp.sum(dec_wide * dec_wide, axis=1).reshape(8, own)
    nsq_two = [nsq_part, swap(nsq_part, "pair")]
    quarter, nsq_two[0], nsq_two[1], at = lax.optimization_barrier((quarter, *nsq_two, at))

    near = gather(act, "y").reshape(256, D)
    far = gather(quarter, ("y", "x")).reshape(256, D)

    def split(value):
        high = value.astype(BF)
        return [high, (value - high.astype(F32)).astype(BF)]

    thresh_level = thresholds.astype(F32) * 0.25

    parts, chunk = 4, D // 4
    encode = call(
        encode_kernel,
        "encode",
        2 * 256 * D * own,
        [((128, own), F32), ((128, own), F32)],
        0,
        [
            pltpu.VMEM((parts, 256, chunk), BF),
            pltpu.VMEM((parts, chunk, own), BF),
            pltpu.VMEM((256, own), F32),
            pltpu.SemaphoreType.DMA((2 * parts,)),
        ],
        2,
    )
    def halves(value):
        split_rows = value.reshape(16, 2, 8, value.shape[1])
        return [
            lax.dynamic_index_in_dim(split_rows, k, 1, False).reshape(128, value.shape[1])
            for k in (pair_at, 1 - pair_at)
        ]

    def features(keep, came):
        pre = keep + came + enc_bias
        return (pre * jax.nn.sigmoid((pre - thresh_level) / smooth_width)).astype(BF)

    keep, send = encode(at, near, enc)
    feats_near = features(keep, swap(send, "pair"))
    nsq_rows = lax.optimization_barrier(
        jnp.concatenate(split(nsq_two[0]) + split(nsq_two[1]), axis=0)
    )
    over = swap(jnp.concatenate([feats_near, nsq_rows], axis=0), "zh")
    dec_held, _ = lax.optimization_barrier((dec_t, feats_near))
    dec_oth = swap(dec_held, "pair")

    part_far = jnp.dot(far, enc, preferred_element_type=F32)
    keep, send = halves(part_far)
    over, keep = lax.optimization_barrier((over, keep))
    feats_far = features(keep, swap(send, "pair"))
    over_far = swap(feats_far, "zh")
    g1 = gather(
        jnp.concatenate([feats_near, over[:128], feats_far, nsq_rows, over[128:]], axis=0), "y"
    )
    over_far, g1 = lax.optimization_barrier((over_far, g1))
    g2 = gather(over_far, "y")

    partial_sums, norm_rows = call(
        decode_kernel,
        "decode",
        2 * tokens * 8 * own * 512,
        [((tokens // 2, 1024), F32), ((64, 8 * own), BF)],
        3,
        [pltpu.VMEM((tokens // 2, 8 * own), BF), pltpu.VMEM((64, 8 * own), F32)],
        limit=40,
    )(at, g1, dec_t, dec_oth)
    (payload,) = call(
        finish_kernel,
        "finish",
        tokens * 4 * own * 512,
        [((tokens // 2, 1024), BF)],
        5,
        [],
        limit=40,
    )(at, g2, dec_t, dec_oth, norm_rows, partial_sums)
    arrived = lax.all_to_all(payload.reshape(32, 8, 1024), LAT, 0, 0)

    cols = [
        halves(lax.dynamic_slice_in_dim(acts, tok_at * width, width, 1)) for acts in (near, far)
    ]
    own_acts = jnp.concatenate([cols[0][0], cols[1][0]], axis=0)
    bias_rows, rest = [], dec_bias
    for _ in range(3):
        bias_rows.append(rest.astype(BF))
        rest = rest - bias_rows[-1].astype(F32)
    bias_rows = jnp.pad(jnp.concatenate(bias_rows, axis=0), ((0, 13), (0, 0)))
    sent = jnp.concatenate([cols[0][1], cols[1][1], bias_rows], axis=0)
    came = swap(sent, "pair")
    pack, stats = call(
        numer_kernel,
        "numer",
        2 * tokens * 8 * own * width,
        [((32, 512), F32), ((2, own), F32)],
        7,
        [pltpu.VMEM((2, 8, own), F32), pltpu.VMEM((8, own), F32)],
        limit=40,
    )(at, g1, g2, dec_t, dec_oth, own_acts, came, dec_bias)
    nsq_own = stats[1]
    mean_sq = (stats[:1] + swap(stats[:1], "pair"))[0] / tokens

    recon_own, recon_his, last = call(
        close_kernel,
        "close",
        1 << 20,
        [((8, width), BF), ((8, width), BF), ((16, 4, 128), F32)],
        2,
        [],
        limit=16,
    )(at, arrived, pack)
    got = lax.all_to_all(last, ("pair",) + TOK, 0, 0, tiled=True)
    recon_came = swap(recon_his, "pair")
    recon = jnp.where(
        pair_at == 0,
        jnp.concatenate([recon_own, recon_came], axis=0),
        jnp.concatenate([recon_came, recon_own], axis=0),
    )
    token_loss = jnp.sum(got[:, 2, :rows], axis=0)
    num_own = jnp.sum(got[:, :2, :], axis=0).reshape(own) / tokens
    scaling = num_own / (nsq_own * mean_sq + tiny_term)
    return (recon[None], token_loss, scaling[None])


def solution(mesh):
    fine = Mesh(mesh.devices.reshape(2, 4, 8, 4, 2), ("pair", "x", "zl", "y", "zh"))
    return jax.shard_map(
        body,
        mesh=fine,
        in_specs=(
            P("pair", TOK, None),
            P("pair", None, LAT + TOK),
            P(LAT + TOK),
            P(LAT + TOK),
            P("pair", LAT, TOK),
            P("pair", TOK),
        ),
        out_specs=(P("pair", LAT, TOK), P(LAT), P("pair", LAT + TOK)),
        check_vma=False,
    )
```

```python
import jax
import jax.numpy as jnp
from jax import lax
from jax.experimental import pallas as pl
from jax.experimental.pallas import tpu as pltpu
from jax.sharding import Mesh, PartitionSpec as P

D = 3584
smooth_width = 0.1
penalty = 0.0001
tiny_term = 1e-06
LAT = ("x", "zl")
TOK = ("y", "zh")
BF = jnp.bfloat16
F32 = jnp.float32
VMEM = pl.BlockSpec(memory_space=pltpu.VMEM)
HBM = pl.BlockSpec(memory_space=pltpu.HBM)
SMEM = pl.BlockSpec(memory_space=pltpu.SMEM)
NT = (((1,), (1,)), ((), ()))


def swap(value, axis):
    return lax.ppermute(value, axis, [(0, 1), (1, 0)])


def gather(value, axes):
    size = lax.axis_size(axes)
    copies = jnp.broadcast_to(value[None], (size,) + value.shape)
    return lax.all_to_all(copies, axes, 0, 0, tiled=False)


def copies_kernel(value_ref, out_hbm, sems):
    copies = [
        pltpu.make_async_copy(value_ref, out_hbm.at[k], sems.at[k])
        for k in range(out_hbm.shape[0])
    ]
    for copy in copies:
        copy.start()
    for copy in copies:
        copy.wait()


def encode_kernel(at_ref, act_hbm, enc_hbm, keep_ref, send_ref, a_ref, enc_ref, v_ref, sems):
    pair_at = at_ref[0]
    count = a_ref.shape[0]
    chunk = a_ref.shape[2]
    loads = []
    for k in range(count):
        span = pl.ds(k * chunk, chunk)
        loads.append(
            (
                pltpu.make_async_copy(act_hbm.at[:, span], a_ref.at[k], sems.at[2 * k]),
                pltpu.make_async_copy(enc_hbm.at[span], enc_ref.at[k], sems.at[2 * k + 1]),
            )
        )
    for pair in loads:
        for copy in pair:
            copy.start()
    for k in range(count):
        for copy in loads[k]:
            copy.wait()
        part = jnp.dot(a_ref[k], enc_ref[k], preferred_element_type=F32)
        if k == 0:
            v_ref[...] = part
        else:
            v_ref[...] += part
    for j in range(16):
        rows = slice(j * 8, (j + 1) * 8)
        kept = pl.multiple_of(j * 16 + pair_at * 8, 8)
        sent = pl.multiple_of(j * 16 + (1 - pair_at) * 8, 8)
        keep_ref[rows, :] = v_ref[pl.ds(kept, 8), :]
        send_ref[rows, :] = v_ref[pl.ds(sent, 8), :]


def norms_of(g1):
    nsq = [jnp.zeros((8, 256), F32)] * 2
    for y in range(4):
        for at in (384, 416):
            rows = g1[y, at : at + 32, :].astype(F32)
            nsq[0] = nsq[0] + (rows[0:8] + rows[8:16])
            nsq[1] = nsq[1] + (rows[16:24] + rows[24:32])
    return nsq


def decode_kernel(
    at_ref, g1, g2, dec_ref, oth_ref, out_ref, f_ref, wide_ref, norm_ref
):
    zh_at = at_ref[1]

    nsq = norms_of(g1)
    norm = (jnp.sqrt(nsq[0]) + jnp.sqrt(nsq[1])) * 0.125
    high = norm.astype(BF).astype(F32)
    wide_ref[...] = jnp.zeros_like(wide_ref)
    for k in range(8):
        wide_ref[0:1, k * 256 : (k + 1) * 256] = high[k : k + 1]
        wide_ref[1:2, k * 256 : (k + 1) * 256] = (norm - high)[k : k + 1]
    norm_ref[...] = wide_ref[...].astype(BF)

    for y in range(4):
        mine = pl.multiple_of((2 * y + zh_at) * 256, 256)
        theirs = pl.multiple_of((2 * y + 1 - zh_at) * 256, 256)
        f_ref[0:128, pl.ds(mine, 256)] = g1[y, 0:128, :]
        f_ref[128:256, pl.ds(theirs, 256)] = g1[y, 128:256, :]
        f_ref[128:256, pl.ds(mine, 256)] = g1[y, 256:384, :]
        f_ref[0:128, pl.ds(theirs, 256)] = g2[y]
    feats = f_ref[...]
    out = []
    for ref in (dec_ref, norm_ref, oth_ref):
        value = lax.dot_general(feats, ref[...], NT, preferred_element_type=F32)
        out.append(value.astype(BF))
    for half in range(2):
        zh = zh_at if half == 0 else 1 - zh_at
        for y in range(4):
            src = slice(half * 128 + y * 32, half * 128 + (y + 1) * 32)
            dst = pl.ds(pl.multiple_of((2 * y + zh) * 32, 32), 32)
            out_ref[dst, 0:448] = out[0][src]
            out_ref[dst, 448:512] = out[1][src]
            out_ref[dst, 512:960] = out[2][src]
            out_ref[dst, 960:1024] = jnp.zeros((32, 64), BF)


def numer_kernel(
    at_ref,
    g1,
    g2,
    dec_ref,
    oth_ref,
    own_ref,
    his_ref,
    bias_ref,
    pack_ref,
    stat_ref,
    num_ref,
    nsq_ref,
):
    zh_at, tok_at, y_at, lat_at = [at_ref[k] for k in range(1, 5)]
    for k, (acts, dec) in enumerate(((own_ref, dec_ref), (his_ref, oth_ref))):
        rows = acts[0:256, :]
        for y in range(4):
            for zh in range(2):
                at = 2 * y + (zh_at if zh == 0 else 1 - zh_at)
                cols = dec[:, pl.ds(pl.multiple_of(at * 256, 256), 256)]
                inner = jnp.dot(rows, cols, preferred_element_type=F32)
                near = g1[y, 0:128, :] if zh == 0 else g2[y]
                far = g1[y, 256:384, :] if zh == 0 else g1[y, 128:256, :]
                both = inner[0:128] * near.astype(F32) + inner[128:256] * far.astype(F32)
                num_ref[k, pl.ds(at, 1), :] = jnp.sum(both, axis=0, keepdims=True)
    pack_ref[0:8, 0:256] = num_ref[0]
    pack_ref[0:8, 256:512] = num_ref[1]

    row = (lat_at // 8) * 32 + (lat_at % 4) * 8
    row = row + jnp.where((lat_at // 4) % 2 == zh_at, 0, 128)
    for k, acts in enumerate((own_ref, his_ref)):
        rows = acts[pl.ds(pl.multiple_of((row // 16) * 16, 16), 16), :].astype(F32)
        kept = jnp.where((row // 8) % 2 == 0, rows[0:8], rows[8:16])
        pack_ref[8 + 8 * k : 16 + 8 * k, 0:448] = kept
    pack_ref[24:25, 0:448] = bias_ref[...]
    rows = his_ref[256:272, :].astype(F32)
    pack_ref[25:26, 0:448] = (rows[0:1] + rows[1:2]) + rows[2:3]

    squares = jnp.zeros((128, 256), F32)
    for rows in (slice(0, 128), slice(256, 384)):
        feats = g1[y_at, rows, :].astype(F32)
        squares = squares + feats * feats
    nsq_ref[...] = norms_of(g1)[0]
    stat_ref[0:1, :] = jnp.sum(squares, axis=0, keepdims=True)
    stat_ref[1:2, :] = nsq_ref[pl.ds(tok_at, 1), :]


def close_kernel(at_ref, arrived_ref, pack_ref, recon_ref, his_recon_ref, last_ref):
    pair_at = at_ref[0]
    total = arrived_ref[0].astype(F32)
    for k in range(1, 32):
        total = total + arrived_ref[k].astype(F32)
    terms = penalty * (total[:, 448:449] + total[:, 449:450])
    for k, out in enumerate((recon_ref, his_recon_ref)):
        recon = total[:, 512 * k : 512 * k + 448] + pack_ref[24 + k : 25 + k, 0:448]
        out[...] = recon.astype(BF)
        residue = pack_ref[8 + 8 * k : 16 + 8 * k, 0:448] - recon
        terms = terms + jnp.sum(residue * residue, axis=1, keepdims=True) / (2.0 * D)
    row = lax.broadcasted_iota(jnp.int32, (8, 128), 0)
    lane = lax.broadcasted_iota(jnp.int32, (8, 128), 1)
    line = jnp.sum(jnp.where(row + pair_at * 8 == lane, terms, 0.0), axis=0, keepdims=True)
    for pair in range(2):
        num = jnp.where(pair_at == pair, pack_ref[0:8, 0:256], pack_ref[0:8, 256:512])
        for k in range(8):
            at = pair * 8 + k
            last_ref[at, 0:1, :] = num[k : k + 1, 0:128]
            last_ref[at, 1:2, :] = num[k : k + 1, 128:256]
            last_ref[at, 2:3, :] = line
            last_ref[at, 3:4, :] = line


def call(kernel, name, flops, outs, count, scratch, outside=0, limit=60):
    return pl.pallas_call(
        kernel,
        out_shape=tuple(jax.ShapeDtypeStruct(shape, kind) for shape, kind in outs),
        in_specs=[SMEM] + [VMEM] * count + [HBM] * outside,
        out_specs=(VMEM,) * len(outs),
        scratch_shapes=scratch,
        compiler_params=pltpu.CompilerParams(vmem_limit_bytes=limit << 20),
        cost_estimate=pl.CostEstimate(
            flops=flops, bytes_accessed=6 << 20, transcendentals=0
        ),
        name=name,
    )


def body(activations, enc_weight, enc_bias, thresholds, dec_weight, dec_bias):
    pair_at = lax.axis_index("pair")
    x_at = lax.axis_index("x")
    zh_at = lax.axis_index("zh")
    tok_at = lax.axis_index(TOK)
    lat_at = lax.axis_index(LAT)
    act = activations[0]
    enc = enc_weight[0]
    dec = dec_weight[0]
    dec_t = dec.T
    own, width = enc.shape[1], dec.shape[1]
    tokens = 8 * act.shape[0]
    rows = tokens // lax.axis_size(LAT)
    at = jnp.stack([pair_at, zh_at, tok_at, lax.axis_index("y"), lat_at]).astype(jnp.int32)

    quarter = swap(lax.dynamic_slice_in_dim(act, x_at * 16, 16, 0), "zh")
    dec_wide = dec.astype(F32)
    nsq_part = jnp.sum(dec_wide * dec_wide, axis=1).reshape(8, own)
    nsq_two = [nsq_part, swap(nsq_part, "pair")]
    quarter, nsq_two[0], nsq_two[1], at = lax.optimization_barrier((quarter, *nsq_two, at))

    (copies,) = pl.pallas_call(
        copies_kernel,
        out_shape=(jax.ShapeDtypeStruct((4,) + act.shape, BF),),
        in_specs=[VMEM],
        out_specs=(HBM,),
        scratch_shapes=[pltpu.SemaphoreType.DMA((4,))],
        compiler_params=pltpu.CompilerParams(vmem_limit_bytes=60 << 20),
        cost_estimate=pl.CostEstimate(
            flops=0, bytes_accessed=2 << 20, transcendentals=0
        ),
        name="copies",
    )(act)
    near = lax.all_to_all(copies, "y", 0, 0, tiled=False).reshape(256, D)
    far = gather(quarter, ("y", "x")).reshape(256, D)

    def split(value):
        high = value.astype(BF)
        return [high, (value - high.astype(F32)).astype(BF)]

    thresh_level = thresholds.astype(F32) * 0.25

    parts, chunk = 4, D // 4
    encode = call(
        encode_kernel,
        "encode",
        2 * 256 * D * own,
        [((128, own), F32), ((128, own), F32)],
        0,
        [
            pltpu.VMEM((parts, 256, chunk), BF),
            pltpu.VMEM((parts, chunk, own), BF),
            pltpu.VMEM((256, own), F32),
            pltpu.SemaphoreType.DMA((2 * parts,)),
        ],
        2,
    )
    def halves(value):
        split_rows = value.reshape(16, 2, 8, value.shape[1])
        return [
            lax.dynamic_index_in_dim(split_rows, k, 1, False).reshape(128, value.shape[1])
            for k in (pair_at, 1 - pair_at)
        ]

    def features(keep, came):
        pre = keep + came + enc_bias
        return (pre * jax.nn.sigmoid((pre - thresh_level) / smooth_width)).astype(BF)

    keep, send = encode(at, near, enc)
    feats_near = features(keep, swap(send, "pair"))
    nsq_rows = lax.optimization_barrier(
        jnp.concatenate(split(nsq_two[0]) + split(nsq_two[1]), axis=0)
    )
    over = swap(jnp.concatenate([feats_near, nsq_rows], axis=0), "zh")
    dec_held, _ = lax.optimization_barrier((dec_t, feats_near))
    dec_oth = swap(dec_held, "pair")

    part_far = jnp.dot(far, enc, preferred_element_type=F32)
    keep, send = halves(part_far)
    over, keep = lax.optimization_barrier((over, keep))
    feats_far = features(keep, swap(send, "pair"))
    over_far = swap(feats_far, "zh")
    g1 = gather(
        jnp.concatenate([feats_near, over[:128], feats_far, nsq_rows, over[128:]], axis=0), "y"
    )
    over_far, g1 = lax.optimization_barrier((over_far, g1))
    g2 = gather(over_far, "y")

    (payload,) = call(
        decode_kernel,
        "decode",
        2 * tokens * 8 * own * 512,
        [((tokens // 2, 1024), BF)],
        4,
        [
            pltpu.VMEM((tokens // 2, 8 * own), BF),
            pltpu.VMEM((64, 8 * own), F32),
            pltpu.VMEM((64, 8 * own), BF),
        ],
        limit=40,
    )(at, g1, g2, dec_t, dec_oth)
    arrived = lax.all_to_all(payload.reshape(32, 8, 1024), LAT, 0, 0)

    cols = [
        halves(lax.dynamic_slice_in_dim(acts, tok_at * width, width, 1)) for acts in (near, far)
    ]
    own_acts = jnp.concatenate([cols[0][0], cols[1][0]], axis=0)
    bias_rows, rest = [], dec_bias
    for _ in range(3):
        bias_rows.append(rest.astype(BF))
        rest = rest - bias_rows[-1].astype(F32)
    bias_rows = jnp.pad(jnp.concatenate(bias_rows, axis=0), ((0, 13), (0, 0)))
    sent = jnp.concatenate([cols[0][1], cols[1][1], bias_rows], axis=0)
    came = swap(sent, "pair")
    pack, stats = call(
        numer_kernel,
        "numer",
        2 * tokens * 8 * own * width,
        [((32, 512), F32), ((2, own), F32)],
        7,
        [pltpu.VMEM((2, 8, own), F32), pltpu.VMEM((8, own), F32)],
        limit=40,
    )(at, g1, g2, dec_t, dec_oth, own_acts, came, dec_bias)
    nsq_own = stats[1]
    mean_sq = (stats[:1] + swap(stats[:1], "pair"))[0] / tokens

    recon_own, recon_his, last = call(
        close_kernel,
        "close",
        1 << 20,
        [((8, width), BF), ((8, width), BF), ((16, 4, 128), F32)],
        2,
        [],
        limit=16,
    )(at, arrived, pack)
    got = lax.all_to_all(last, ("pair",) + TOK, 0, 0, tiled=True)
    recon_came = swap(recon_his, "pair")
    recon = jnp.where(
        pair_at == 0,
        jnp.concatenate([recon_own, recon_came], axis=0),
        jnp.concatenate([recon_came, recon_own], axis=0),
    )
    token_loss = jnp.sum(got[:, 2, :rows], axis=0)
    num_own = jnp.sum(got[:, :2, :], axis=0).reshape(own) / tokens
    scaling = num_own / (nsq_own * mean_sq + tiny_term)
    return (recon[None], token_loss, scaling[None])


def solution(mesh):
    fine = Mesh(mesh.devices.reshape(2, 4, 8, 4, 2), ("pair", "x", "zl", "y", "zh"))
    return jax.shard_map(
        body,
        mesh=fine,
        in_specs=(
            P("pair", TOK, None),
            P("pair", None, LAT + TOK),
            P(LAT + TOK),
            P(LAT + TOK),
            P("pair", LAT, TOK),
            P("pair", TOK),
        ),
        out_specs=(P("pair", LAT, TOK), P(LAT), P("pair", LAT + TOK)),
        check_vma=False,
    )
```

```python
import jax
import jax.numpy as jnp
from jax import lax
from jax.experimental import pallas as pl
from jax.experimental.pallas import tpu as pltpu
from jax.sharding import Mesh, PartitionSpec as P

D = 3584
smooth_width = 0.1
penalty = 0.0001
tiny_term = 1e-06
LAT = ("x", "zl")
TOK = ("y", "zh")
BF = jnp.bfloat16
F32 = jnp.float32
VMEM = pl.BlockSpec(memory_space=pltpu.VMEM)
HBM = pl.BlockSpec(memory_space=pltpu.HBM)
SMEM = pl.BlockSpec(memory_space=pltpu.SMEM)
NT = (((1,), (1,)), ((), ()))


def swap(value, axis):
    return lax.ppermute(value, axis, [(0, 1), (1, 0)])


def gather(value, axes):
    size = lax.axis_size(axes)
    copies = jnp.broadcast_to(value[None], (size,) + value.shape)
    return lax.all_to_all(copies, axes, 0, 0, tiled=False)


def copies_kernel(value_ref, out_hbm, sems):
    copies = [
        pltpu.make_async_copy(value_ref, out_hbm.at[k], sems.at[k])
        for k in range(out_hbm.shape[0])
    ]
    for copy in copies:
        copy.start()
    for copy in copies:
        copy.wait()


def encode_kernel(at_ref, act_hbm, enc_hbm, keep_ref, send_ref, a_ref, enc_ref, v_ref, sems):
    pair_at = at_ref[0]
    count = a_ref.shape[0]
    chunk = a_ref.shape[2]
    loads = []
    for k in range(count):
        span = pl.ds(k * chunk, chunk)
        loads.append(
            (
                pltpu.make_async_copy(act_hbm.at[:, span], a_ref.at[k], sems.at[2 * k]),
                pltpu.make_async_copy(enc_hbm.at[span], enc_ref.at[k], sems.at[2 * k + 1]),
            )
        )
    for pair in loads:
        for copy in pair:
            copy.start()
    for k in range(count):
        for copy in loads[k]:
            copy.wait()
        part = jnp.dot(a_ref[k], enc_ref[k], preferred_element_type=F32)
        if k == 0:
            v_ref[...] = part
        else:
            v_ref[...] += part
    for j in range(16):
        rows = slice(j * 8, (j + 1) * 8)
        kept = pl.multiple_of(j * 16 + pair_at * 8, 8)
        sent = pl.multiple_of(j * 16 + (1 - pair_at) * 8, 8)
        keep_ref[rows, :] = v_ref[pl.ds(kept, 8), :]
        send_ref[rows, :] = v_ref[pl.ds(sent, 8), :]


def norms_of(g1):
    nsq = [jnp.zeros((8, 256), F32)] * 2
    for y in range(4):
        for at in (384, 416):
            rows = g1[y, at : at + 32, :].astype(F32)
            nsq[0] = nsq[0] + (rows[0:8] + rows[8:16])
            nsq[1] = nsq[1] + (rows[16:24] + rows[24:32])
    return nsq


def decode_kernel(
    at_ref, g1, g2, dec_ref, oth_ref, out_ref, f_ref, wide_ref, norm_ref
):
    zh_at = at_ref[1]

    nsq = norms_of(g1)
    norm = (jnp.sqrt(nsq[0]) + jnp.sqrt(nsq[1])) * 0.125
    high = norm.astype(BF).astype(F32)
    wide_ref[...] = jnp.zeros_like(wide_ref)
    for k in range(8):
        wide_ref[0:1, k * 256 : (k + 1) * 256] = high[k : k + 1]
        wide_ref[1:2, k * 256 : (k + 1) * 256] = (norm - high)[k : k + 1]
    norm_ref[...] = wide_ref[...].astype(BF)

    for y in range(4):
        mine = pl.multiple_of((2 * y + zh_at) * 256, 256)
        theirs = pl.multiple_of((2 * y + 1 - zh_at) * 256, 256)
        f_ref[0:128, pl.ds(mine, 256)] = g1[y, 0:128, :]
        f_ref[128:256, pl.ds(theirs, 256)] = g1[y, 128:256, :]
        f_ref[128:256, pl.ds(mine, 256)] = g1[y, 256:384, :]
        f_ref[0:128, pl.ds(theirs, 256)] = g2[y]
    feats = f_ref[...]
    out = []
    for ref in (dec_ref, norm_ref, oth_ref):
        value = lax.dot_general(feats, ref[...], NT, preferred_element_type=F32)
        out.append(value.astype(BF))
    for half in range(2):
        zh = zh_at if half == 0 else 1 - zh_at
        for y in range(4):
            src = slice(half * 128 + y * 32, half * 128 + (y + 1) * 32)
            dst = pl.ds(pl.multiple_of((2 * y + zh) * 32, 32), 32)
            out_ref[dst, 0:448] = out[0][src]
            out_ref[dst, 448:512] = out[1][src]
            out_ref[dst, 512:960] = out[2][src]
            out_ref[dst, 960:1024] = jnp.zeros((32, 64), BF)


def numer_kernel(
    at_ref,
    g1,
    g2,
    dec_ref,
    oth_ref,
    own_ref,
    his_ref,
    bias_ref,
    pack_ref,
    stat_ref,
    num_ref,
    nsq_ref,
):
    zh_at, tok_at, y_at, lat_at = [at_ref[k] for k in range(1, 5)]
    for k, (acts, dec) in enumerate(((own_ref, dec_ref), (his_ref, oth_ref))):
        rows = acts[0:256, :]
        for y in range(4):
            for zh in range(2):
                at = 2 * y + (zh_at if zh == 0 else 1 - zh_at)
                cols = dec[:, pl.ds(pl.multiple_of(at * 256, 256), 256)]
                inner = jnp.dot(rows, cols, preferred_element_type=F32)
                near = g1[y, 0:128, :] if zh == 0 else g2[y]
                far = g1[y, 256:384, :] if zh == 0 else g1[y, 128:256, :]
                both = inner[0:128] * near.astype(F32) + inner[128:256] * far.astype(F32)
                num_ref[k, pl.ds(at, 1), :] = jnp.sum(both, axis=0, keepdims=True)
    pack_ref[0:8, 0:256] = num_ref[0]
    pack_ref[0:8, 256:512] = num_ref[1]

    row = (lat_at // 8) * 32 + (lat_at % 4) * 8
    row = row + jnp.where((lat_at // 4) % 2 == zh_at, 0, 128)
    for k, acts in enumerate((own_ref, his_ref)):
        rows = acts[pl.ds(pl.multiple_of((row // 16) * 16, 16), 16), :].astype(F32)
        kept = jnp.where((row // 8) % 2 == 0, rows[0:8], rows[8:16])
        pack_ref[8 + 8 * k : 16 + 8 * k, 0:448] = kept
    pack_ref[24:25, 0:448] = bias_ref[...]
    rows = his_ref[256:272, :].astype(F32)
    pack_ref[25:26, 0:448] = (rows[0:1] + rows[1:2]) + rows[2:3]

    squares = jnp.zeros((128, 256), F32)
    for rows in (slice(0, 128), slice(256, 384)):
        feats = g1[y_at, rows, :].astype(F32)
        squares = squares + feats * feats
    nsq_ref[...] = norms_of(g1)[0]
    stat_ref[0:1, :] = jnp.sum(squares, axis=0, keepdims=True)
    stat_ref[1:2, :] = nsq_ref[pl.ds(tok_at, 1), :]


def close_kernel(at_ref, arrived_ref, pack_ref, recon_ref, his_recon_ref, last_ref):
    pair_at = at_ref[0]
    total = arrived_ref[0].astype(F32)
    for k in range(1, 32):
        total = total + arrived_ref[k].astype(F32)
    terms = penalty * (total[:, 448:449] + total[:, 449:450])
    for k, out in enumerate((recon_ref, his_recon_ref)):
        recon = total[:, 512 * k : 512 * k + 448] + pack_ref[24 + k : 25 + k, 0:448]
        out[...] = recon.astype(BF)
        residue = pack_ref[8 + 8 * k : 16 + 8 * k, 0:448] - recon
        terms = terms + jnp.sum(residue * residue, axis=1, keepdims=True) / (2.0 * D)
    row = lax.broadcasted_iota(jnp.int32, (8, 128), 0)
    lane = lax.broadcasted_iota(jnp.int32, (8, 128), 1)
    line = jnp.sum(jnp.where(row + pair_at * 8 == lane, terms, 0.0), axis=0, keepdims=True)
    for pair in range(2):
        num = jnp.where(pair_at == pair, pack_ref[0:8, 0:256], pack_ref[0:8, 256:512])
        for k in range(8):
            at = pair * 8 + k
            last_ref[at, 0:1, :] = num[k : k + 1, 0:128]
            last_ref[at, 1:2, :] = num[k : k + 1, 128:256]
            last_ref[at, 2:3, :] = line
            last_ref[at, 3:4, :] = line


def call(kernel, name, flops, outs, count, scratch, outside=0, limit=60):
    return pl.pallas_call(
        kernel,
        out_shape=tuple(jax.ShapeDtypeStruct(shape, kind) for shape, kind in outs),
        in_specs=[SMEM] + [VMEM] * count + [HBM] * outside,
        out_specs=(VMEM,) * len(outs),
        scratch_shapes=scratch,
        compiler_params=pltpu.CompilerParams(vmem_limit_bytes=limit << 20),
        cost_estimate=pl.CostEstimate(
            flops=flops, bytes_accessed=6 << 20, transcendentals=0
        ),
        name=name,
    )


def body(activations, enc_weight, enc_bias, thresholds, dec_weight, dec_bias):
    pair_at = lax.axis_index("pair")
    x_at = lax.axis_index("x")
    zh_at = lax.axis_index("zh")
    tok_at = lax.axis_index(TOK)
    lat_at = lax.axis_index(LAT)
    act = activations[0]
    enc = enc_weight[0]
    dec = dec_weight[0]
    dec_t = dec.T
    own, width = enc.shape[1], dec.shape[1]
    tokens = 8 * act.shape[0]
    rows = tokens // lax.axis_size(LAT)
    at = jnp.stack([pair_at, zh_at, tok_at, lax.axis_index("y"), lat_at]).astype(jnp.int32)

    quarter = swap(lax.dynamic_slice_in_dim(act, x_at * 16, 16, 0), "zh")
    dec_wide = dec.astype(F32)
    nsq_part = jnp.sum(dec_wide * dec_wide, axis=1).reshape(8, own)
    nsq_two = [nsq_part, swap(nsq_part, "pair")]
    quarter, nsq_two[0], nsq_two[1], at = lax.optimization_barrier((quarter, *nsq_two, at))

    (copies,) = pl.pallas_call(
        copies_kernel,
        out_shape=(jax.ShapeDtypeStruct((4,) + act.shape, BF),),
        in_specs=[VMEM],
        out_specs=(HBM,),
        scratch_shapes=[pltpu.SemaphoreType.DMA((4,))],
        compiler_params=pltpu.CompilerParams(vmem_limit_bytes=60 << 20),
        cost_estimate=pl.CostEstimate(
            flops=0, bytes_accessed=2 << 20, transcendentals=0
        ),
        name="copies",
    )(act)
    near = lax.all_to_all(copies, "y", 0, 0, tiled=False).reshape(256, D)
    far = gather(quarter, ("y", "x")).reshape(256, D)

    def split(value):
        high = value.astype(BF)
        return [high, (value - high.astype(F32)).astype(BF)]

    thresh_level = thresholds.astype(F32) * 0.25

    parts, chunk = 4, D // 4
    encode = call(
        encode_kernel,
        "encode",
        2 * 256 * D * own,
        [((128, own), F32), ((128, own), F32)],
        0,
        [
            pltpu.VMEM((parts, 256, chunk), BF),
            pltpu.VMEM((parts, chunk, own), BF),
            pltpu.VMEM((256, own), F32),
            pltpu.SemaphoreType.DMA((2 * parts,)),
        ],
        2,
    )
    def halves(value):
        split_rows = value.reshape(16, 2, 8, value.shape[1])
        return [
            lax.dynamic_index_in_dim(split_rows, k, 1, False).reshape(128, value.shape[1])
            for k in (pair_at, 1 - pair_at)
        ]

    def features(keep, came):
        pre = keep + came + enc_bias
        return (pre * jax.nn.sigmoid((pre - thresh_level) / smooth_width)).astype(BF)

    keep, send = encode(at, near, enc)
    feats_near = features(keep, swap(send, "pair"))
    nsq_rows = lax.optimization_barrier(
        jnp.concatenate(split(nsq_two[0]) + split(nsq_two[1]), axis=0)
    )
    over = swap(jnp.concatenate([feats_near, nsq_rows], axis=0), "zh")
    dec_held, _ = lax.optimization_barrier((dec_t, feats_near))
    dec_oth = swap(dec_held, "pair")

    part_far = jnp.dot(far, enc, preferred_element_type=F32)
    keep, send = halves(part_far)
    over, keep = lax.optimization_barrier((over, keep))
    feats_far = features(keep, swap(send, "pair"))
    over_far = swap(feats_far, "zh")
    g1 = gather(
        jnp.concatenate([feats_near, over[:128], feats_far, nsq_rows, over[128:]], axis=0), "y"
    )
    over_far, g1 = lax.optimization_barrier((over_far, g1))
    g2 = gather(over_far, "y")

    (payload,) = call(
        decode_kernel,
        "decode",
        2 * tokens * 8 * own * 512,
        [((tokens // 2, 1024), BF)],
        4,
        [
            pltpu.VMEM((tokens // 2, 8 * own), BF),
            pltpu.VMEM((64, 8 * own), F32),
            pltpu.VMEM((64, 8 * own), BF),
        ],
        limit=40,
    )(at, g1, g2, dec_t, dec_oth)
    arrived = lax.all_to_all(payload.reshape(32, 8, 1024), LAT, 0, 0)

    cols = [
        halves(lax.dynamic_slice_in_dim(acts, tok_at * width, width, 1)) for acts in (near, far)
    ]
    own_acts = jnp.concatenate([cols[0][0], cols[1][0]], axis=0)
    bias_rows, rest = [], dec_bias
    for _ in range(3):
        bias_rows.append(rest.astype(BF))
        rest = rest - bias_rows[-1].astype(F32)
    bias_rows = jnp.pad(jnp.concatenate(bias_rows, axis=0), ((0, 13), (0, 0)))
    sent = jnp.concatenate([cols[0][1], cols[1][1], bias_rows], axis=0)
    came = swap(sent, "pair")
    pack, stats = call(
        numer_kernel,
        "numer",
        2 * tokens * 8 * own * width,
        [((32, 512), F32), ((2, own), F32)],
        7,
        [pltpu.VMEM((2, 8, own), F32), pltpu.VMEM((8, own), F32)],
        limit=40,
    )(at, g1, g2, dec_t, dec_oth, own_acts, came, dec_bias)
    nsq_own = stats[1]
    mean_sq = (stats[:1] + swap(stats[:1], "pair"))[0] / tokens
    arrived, mean_sq = lax.optimization_barrier((arrived, mean_sq))

    recon_own, recon_his, last = call(
        close_kernel,
        "close",
        1 << 20,
        [((8, width), BF), ((8, width), BF), ((16, 4, 128), F32)],
        2,
        [],
        limit=16,
    )(at, arrived, pack)
    got = lax.all_to_all(last, ("pair",) + TOK, 0, 0, tiled=True)
    recon_came = swap(recon_his, "pair")
    recon = jnp.where(
        pair_at == 0,
        jnp.concatenate([recon_own, recon_came], axis=0),
        jnp.concatenate([recon_came, recon_own], axis=0),
    )
    token_loss = jnp.sum(got[:, 2, :rows], axis=0)
    num_own = jnp.sum(got[:, :2, :], axis=0).reshape(own) / tokens
    scaling = num_own / (nsq_own * mean_sq + tiny_term)
    return (recon[None], token_loss, scaling[None])


def solution(mesh):
    fine = Mesh(mesh.devices.reshape(2, 4, 8, 4, 2), ("pair", "x", "zl", "y", "zh"))
    return jax.shard_map(
        body,
        mesh=fine,
        in_specs=(
            P("pair", TOK, None),
            P("pair", None, LAT + TOK),
            P(LAT + TOK),
            P(LAT + TOK),
            P("pair", LAT, TOK),
            P("pair", TOK),
        ),
        out_specs=(P("pair", LAT, TOK), P(LAT), P("pair", LAT + TOK)),
        check_vma=False,
    )
```
